128 devices in a mesh: ctx: 16 (over y, z_lo, core), tp: 8 (over x, z_hi).
Axes of the slice: x: 4, y: 4, z: 4 (z_hi: 2, z_lo: 2; z = z_hi * 2 + z_lo), core: 2. Of those that a mesh axis runs over, the one named last changes fastest.
Arguments:
- queries: bfloat16 [4096, 8192], P('ctx', 'tp'), may hold values from -6 to 6
- key_states: bfloat16 [4096, 1024], P('ctx', 'tp'), may hold values from -6 to 6
- value_states: bfloat16 [4096, 1024], P('ctx', 'tp'), may hold values from -6 to 6
- attn_output: bfloat16 [4096, 8192], P('ctx', 'tp'), may hold values from -3 to 3
- output_grad: bfloat16 [4096, 8192], P('ctx', 'tp'), may hold values from -16 to 16
- log_norms: float32 [64, 4096], P('tp', 'ctx')
- layer_input: bfloat16 [4096, 8192], P('ctx', 'tp'), may hold values from -6 to 6
- doc_lengths: int32 [16], replicated, may hold values from 1 to 2048, as said below
Outputs:
- query_grad: bfloat16 [4096, 8192], P('ctx', 'tp')
- key_weight_grad: float32 [8192, 1024], P('ctx', 'tp')
- value_weight_grad: float32 [8192, 1024], P('ctx', 'tp')
The draws below stay inside these ranges and needn't reach their ends.
Inputs may be any that keep to these rules, and one draw needn't show every extreme that they name: `doc_lengths`: the 16 lengths sum to 4096; the first document is exactly 2048 tokens long.
All inputs are finite; a program needn't handle non-finite values.
Results may differ from the reference program's by a relative error of at most 0.006.
Values may be sent and summed in bfloat16 or wider, within the bound.
No kernel may reach another device: no remote copies, remote signals or barrier semaphores. Data moves between devices by JAX's collectives and lax.ppermute only.
A program may use at most 64 MiB of HBM per device.

```python
import math
import jax
import jax.numpy as jnp
from jax import lax

D = 8192
QH = 64
KVH = 8
HD = 128
NDOC = 16
TOKENS = 4096


def packed_lengths(base_key):
    doc_key = jax.random.fold_in(base_key, 7)
    remaining = TOKENS - TOKENS // 2
    shuffled = jax.random.permutation(doc_key, remaining - 1).astype(jnp.int32) + 1
    cut_points = jnp.sort(shuffled[:NDOC - 2])
    boundaries = jnp.concatenate([jnp.zeros((1,), jnp.int32), cut_points, jnp.full((1,), remaining, jnp.int32)])
    short_lengths = boundaries[1:] - boundaries[:-1]
    return jnp.concatenate([jnp.full((1,), TOKENS // 2, jnp.int32), short_lengths]).astype(jnp.int32)


def draw_doc_lengths(key, part):
    return packed_lengths(key)


def draw_log_norms(key, part):
    doc_lengths = packed_lengths(key)
    doc_ends = jnp.cumsum(doc_lengths).astype(jnp.int32)
    positions = jnp.arange(TOKENS, dtype=jnp.int32)
    first_keys = jnp.max(jnp.where(doc_ends[None, :] <= positions[:, None], doc_ends[None, :], 0), axis=1)
    counts = (positions - first_keys + 1).astype(jnp.float32)
    noise_key = jax.random.fold_in(key, 11)
    noise = jax.random.uniform(noise_key, (QH, TOKENS), jnp.float32, 0.3, 1.5)
    return (jnp.log(counts)[None, :] + noise).astype(jnp.float32)


def strengthened(entries, rng, source, target, blocks, factor):
    owner, partner = [(jnp.arange(entries.shape[dim]) // (entries.shape[dim] // blocks)).reshape([-1 if axis == dim else 1 for axis in range(entries.ndim)]) for dim in (source, target)]
    chosen = jax.random.permutation(rng, blocks)[partner]
    strong = (owner == chosen) | (owner == (partner + blocks // 2) % blocks)
    return jnp.where(strong, factor * entries, entries)


def level_of(own_key, extent, cuts, low, largest):
    def one(dim, parts):
        steps = jax.random.uniform(jax.random.fold_in(jax.random.fold_in(own_key, 6), dim), (parts,), jnp.float32, low / len(cuts), largest / len(cuts))
        return jnp.repeat(jnp.exp(steps), extent[dim] // parts).reshape((-1,) + (1,) * (len(extent) - dim - 1))

    loudness = one(*cuts[0])
    for cut in cuts[1:]:
        loudness = loudness * one(*cut)
    return loudness


def gaussian(own_key, shape, scale, limit, cuts=(), kind=jnp.bfloat16):
    level = level_of(own_key, shape, cuts, -0.22, 0.18) if cuts else 1.0
    entries = jax.random.normal(own_key, shape, jnp.float32) * scale * level
    return jnp.minimum(jnp.maximum(entries, -limit), limit).astype(kind)


def heavy_noise(key, shape, spread, bound, shards, heavy, kind=jnp.bfloat16):
    array = spread * jax.random.normal(key, shape, jnp.float32)
    if shards:
        array = array * level_of(key, shape, shards, -0.22, 0.18)
    return jnp.clip(strengthened(array, jax.random.fold_in(key, 3), *heavy), -bound, bound).astype(kind)


def setup_inputs(seed: int = 0) -> dict:
    key_list = jax.random.split(jax.random.key(seed), 9)
    queries = gaussian(key_list[0], (TOKENS, QH * HD), 1.0, 6.0, ((0, 16), (1, 8)))
    key_states = gaussian(key_list[1], (TOKENS, KVH * HD), 1.0, 6.0, ((0, 16), (1, 8)))
    value_states = gaussian(key_list[2], (TOKENS, KVH * HD), 1.0, 6.0, ((0, 16), (1, 8)))
    attn_output = gaussian(key_list[3], (TOKENS, QH * HD), 0.5, 3.0, ((0, 16), (1, 8)))
    output_grad = gaussian(key_list[4], (TOKENS, QH * HD), 4.0, 16.0, ((0, 16), (1, 8)))
    log_norms = draw_log_norms(jax.random.fold_in(key_list[8], 71), 0)
    layer_input = heavy_noise(key_list[6], (TOKENS, D), 1.0, 6.0, ((0, 16), (1, 8)), (0, 1, 16, 2.0))
    doc_lengths = draw_doc_lengths(jax.random.fold_in(key_list[8], 71), 0)
    return {"queries": queries, "key_states": key_states, "value_states": value_states, "attn_output": attn_output, "output_grad": output_grad, "log_norms": log_norms, "layer_input": layer_input, "doc_lengths": doc_lengths}


def doc_first(doc_lengths, positions):
    doc_ends = jnp.cumsum(doc_lengths).astype(jnp.int32)
    return lax.optimization_barrier(jnp.max(jnp.where(doc_ends[None, :] <= positions[:, None], doc_ends[None, :], 0), axis=1)).astype(jnp.int32)

def reference(queries, key_states, value_states, attn_output, output_grad, log_norms, layer_input, doc_lengths):
    seq_length = queries.shape[0]
    group_size = QH // KVH
    score_scale = 1.0 / math.sqrt(HD)
    positions = jnp.arange(seq_length, dtype=jnp.int32)
    first_keys = doc_first(doc_lengths, positions)
    visible = (positions[None, :] <= positions[:, None]) & (positions[None, :] >= first_keys[:, None])
    query_heads = queries.reshape(seq_length, KVH, group_size, HD).transpose(1, 2, 0, 3)
    grad_heads = output_grad.reshape(seq_length, KVH, group_size, HD).transpose(1, 2, 0, 3)
    out_heads = attn_output.reshape(seq_length, KVH, group_size, HD).transpose(1, 2, 0, 3)
    norm_heads = log_norms.reshape(KVH, group_size, seq_length)
    key_heads = key_states.reshape(seq_length, KVH, HD).transpose(1, 0, 2)
    value_heads = value_states.reshape(seq_length, KVH, HD).transpose(1, 0, 2)

    def one_group(group_items):
        query_group, grad_group, out_group, norm_group, key_group, value_group = group_items

        def one_head(carried, head_items):
            query_one, grad_one, out_one, norm_one = head_items
            row_dots = lax.optimization_barrier(jnp.sum(grad_one.astype(jnp.float32) * out_one.astype(jnp.float32), axis=1))
            scores = jnp.dot(query_one, key_group.T, preferred_element_type=jnp.float32) * score_scale
            probs = jnp.where(visible, jnp.exp(scores - norm_one[:, None]), jnp.float32(0.0))
            probs_low = probs.astype(jnp.bfloat16)
            value_term = jnp.dot(probs_low.T, grad_one, preferred_element_type=jnp.float32)
            prob_grad = jnp.dot(grad_one, value_group.T, preferred_element_type=jnp.float32)
            score_grad = (probs * (prob_grad - row_dots[:, None])).astype(jnp.bfloat16)
            query_term = jnp.dot(score_grad, key_group, preferred_element_type=jnp.float32) * score_scale
            key_term = jnp.dot(score_grad.T, query_one, preferred_element_type=jnp.float32)
            return ((carried[0] + key_term, carried[1] + value_term), query_term.astype(jnp.bfloat16))
        start_sums = (jnp.zeros((seq_length, HD), jnp.float32), jnp.zeros((seq_length, HD), jnp.float32))
        (key_sum, value_sum), query_part = lax.scan(one_head, start_sums, (query_group, grad_group, out_group, norm_group))
        return (query_part, key_sum, value_sum)
    query_part, key_sum, value_sum = lax.map(one_group, (query_heads, grad_heads, out_heads, norm_heads, key_heads, value_heads))
    query_grad = query_part.transpose(2, 0, 1, 3).reshape(seq_length, QH * HD)
    key_low = (key_sum * score_scale).astype(jnp.bfloat16).transpose(1, 0, 2).reshape(seq_length, KVH * HD)
    value_low = value_sum.astype(jnp.bfloat16).transpose(1, 0, 2).reshape(seq_length, KVH * HD)
    key_weight_grad = jnp.dot(layer_input.T, key_low, preferred_element_type=jnp.float32)
    value_weight_grad = jnp.dot(layer_input.T, value_low, preferred_element_type=jnp.float32)
    return (query_grad, key_weight_grad, value_weight_grad)
```

```python
import functools
import itertools
import math

import jax
import jax.numpy as jnp
from jax import lax
from jax.experimental import pallas as pl
from jax.experimental.pallas import tpu as pltpu
from jax.sharding import PartitionSpec as P

HD = 128
HEADS = 8
ROWS = 256
WIDTH = HEADS * HD
SCALE = 1.0 / math.sqrt(HD)
LOG2E = math.log2(math.e)
AXES = ("ctx", "tp")
STEP_HEADS = 2
VMEM = 56 * 1024 * 1024

f32 = jnp.float32
bf16 = jnp.bfloat16


def linear(x, y, z, core):
    zh, zl = divmod(z, 2)
    return ((y * 2 + zl) * 2 + core) * 8 + x * 2 + zh


def route(target):
    pairs = []
    for x, y, z, core in itertools.product(range(4), range(4), range(4), range(2)):
        to = target(x, y, z, core)
        if to is not None:
            pairs.append((linear(x, y, z, core), linear(*to)))
    return pairs


def send(value, target):
    return lax.ppermute(value, AXES, route(target))


def other_core(x, y, z, core):
    return (x, y, z, 1 - core)


def shifted(dx=0, dy=0, dz=0):
    return lambda x, y, z, core: ((x + dx) % 4, (y + dy) % 4, (z + dz) % 4, core)


def other_zl(x, y, z, core):
    return (x, y, z ^ 1, core)


def spread(x, y, z, core):
    zh, zl = divmod(z, 2)
    return ((x + y) % 4, x, zl * 2 + zh, core)


def within_half(flip, later):
    def target(x, y, z, core):
        place = (y % 2) * 2 + z % 2
        to = place ^ flip
        if (to > place) != later:
            return None
        return (x, y - y % 2 + to // 2, z - z % 2 + to % 2, core)

    return target


def nt(a, b):
    return lax.dot_general(a, b, (((1,), (1,)), ((), ())), preferred_element_type=f32)


def nn(a, b):
    return lax.dot_general(a, b, (((1,), (0,)), ((), ())), preferred_element_type=f32)


def tn(a, b):
    return lax.dot_general(a, b, (((0,), (0,)), ((), ())), preferred_element_type=f32)


def dots_kernel(do_ref, out_ref, ln_ref, aux_ref):
    for h in range(HEADS):
        cols = slice(h * HD, (h + 1) * HD)
        prod = do_ref[:, cols].astype(f32) * out_ref[:, cols].astype(f32)
        aux_ref[h : h + 1, :] = jnp.sum(prod.T, axis=0, keepdims=True)
    aux_ref[HEADS:, :] = ln_ref[...] * LOG2E


def row_aux(output_grad, attn_output, log_norms):
    return pl.pallas_call(
        dots_kernel,
        out_shape=jax.ShapeDtypeStruct((2 * HEADS, ROWS), f32),
        compiler_params=pltpu.CompilerParams(vmem_limit_bytes=VMEM),
        cost_estimate=pl.CostEstimate(flops=2 * ROWS * WIDTH, bytes_accessed=4 * ROWS * WIDTH, transcendentals=0),
    )(output_grad, attn_output, log_norms)


def attention_kernel(count, has_sum, *refs):
    (blocks, kv_ref, first_ref, aux_refs, q_refs, do_refs) = (
        refs[0], refs[1], refs[2:4], refs[4:6], refs[6:8], refs[8:10],
    )
    rest = list(refs[10:])
    sums = [rest.pop(0), rest.pop(0)] if has_sum else None
    dq_refs = [rest.pop(0), rest.pop(0)]
    dkv_ref, dk_acc, dv_acc = rest
    step = pl.program_id(0)

    @pl.when(step == 0)
    def _():
        dk_acc[...] = jnp.zeros_like(dk_acc)
        dv_acc[...] = jnp.zeros_like(dv_acc)

    keys = count * ROWS
    k = kv_ref[:, :HD]
    v = kv_ref[:, HD:]
    offset = lax.broadcasted_iota(jnp.int32, (ROWS, 1), 0)
    key_pos = [blocks[i] * ROWS + offset for i in range(count)]
    key_pos = key_pos[0] if count == 1 else jnp.concatenate(key_pos, axis=0)
    lane = lax.broadcasted_iota(jnp.int32, (1, ROWS), 1)
    for i in range(2):
        query_pos = blocks[count + i] * ROWS + lane
        visible = (key_pos <= query_pos) & (key_pos >= first_refs_row(first_ref[i]))
        for j in range(STEP_HEADS):
            cols = slice(j * HD, (j + 1) * HD)
            h = step * STEP_HEADS + j
            q = q_refs[i][:, cols]
            do = do_refs[i][:, cols]
            dots = aux_refs[i][pl.ds(h, 1), :]
            norm = aux_refs[i][pl.ds(HEADS + h, 1), :]
            p = jnp.where(visible, jnp.exp2(nt(k, q) * (SCALE * LOG2E) - norm), 0.0)
            dv_acc[...] += nn(p.astype(bf16), do)
            ds = (p * (nt(v, do) - dots)).astype(bf16)
            dk_acc[...] += nn(ds, q)
            dq = tn(ds, k)
            if has_sum:
                dq = dq + sums[i][:, cols]
            dq_refs[i][:, cols] = dq.astype(dq_refs[i].dtype)

    @pl.when(step == pl.num_programs(0) - 1)
    def _():
        dkv_ref[:, :HD] = dk_acc[...].astype(dkv_ref.dtype)
        dkv_ref[:, HD:] = dv_acc[...].astype(dkv_ref.dtype)


def first_refs_row(ref):
    return ref[0:1, :]


def attention(blocks, kv, first, aux, q, do, sums, dq_types, dkv_type):
    count = kv.shape[0] // ROWS
    whole = lambda a: pl.BlockSpec(a.shape, lambda s, b: (0,) * a.ndim)
    heads = pl.BlockSpec((ROWS, STEP_HEADS * HD), lambda s, b: (0, s))
    operands = [kv, *first, *aux, *q, *do, *(sums or ())]
    specs = [whole(kv), *map(whole, first), *map(whole, aux)] + [heads] * (len(operands) - 5)


    return pl.pallas_call(
        functools.partial(attention_kernel, count, sums is not None),
        out_shape=(
            jax.ShapeDtypeStruct((ROWS, WIDTH), dq_types[0]),
            jax.ShapeDtypeStruct((ROWS, WIDTH), dq_types[1]),
            jax.ShapeDtypeStruct((count * ROWS, 2 * HD), dkv_type),
        ),
        grid_spec=pltpu.PrefetchScalarGridSpec(
            num_scalar_prefetch=1,
            grid=(HEADS // STEP_HEADS,),
            in_specs=specs,
            out_specs=[heads, heads, pl.BlockSpec((count * ROWS, 2 * HD), lambda s, b: (0, 0))],
            scratch_shapes=[pltpu.VMEM((count * ROWS, HD), f32)] * 2,
        ),
        compiler_params=pltpu.CompilerParams(vmem_limit_bytes=VMEM),
        cost_estimate=pl.CostEstimate(
            flops=count * 4 * 5 * 2 * ROWS * ROWS * WIDTH,
            bytes_accessed=12 * ROWS * WIDTH,
            transcendentals=count * 2 * ROWS * ROWS * HEADS,
        ),
    )(blocks, *operands)


def weights_kernel(where, *refs):
    l_refs, d_refs, (out_ref, d_all) = refs[:8], refs[8:12], refs[12:]

    @pl.when(pl.program_id(0) == 0)
    def _():
        for r in range(4):
            for half in range(2):
                d_all[r * 2 + half] = d_refs[r][half * ROWS : (half + 1) * ROWS, :].T

    total = None
    for s in range(4):
        for j in range(2):
            term = nn(d_all[where[s] * 2 + where[4 + j]], l_refs[s * 2 + j][...])
            total = term if total is None else total + term
    out_ref[...] = total


def weights(where, l_blocks, d_blocks):
    tile = 256
    return pl.pallas_call(
        weights_kernel,
        out_shape=jax.ShapeDtypeStruct((2 * HD, WIDTH), f32),
        grid_spec=pltpu.PrefetchScalarGridSpec(
            num_scalar_prefetch=1,
            grid=(WIDTH // tile,),
            in_specs=[pl.BlockSpec((ROWS, tile), lambda s, w: (0, s))] * 8
            + [pl.BlockSpec((2 * ROWS, 2 * HD), lambda s, w: (0, 0))] * 4,
            out_specs=pl.BlockSpec((2 * HD, tile), lambda s, w: (0, s)),
            scratch_shapes=[pltpu.VMEM((8, 2 * HD, ROWS), bf16)],
        ),
        compiler_params=pltpu.CompilerParams(vmem_limit_bytes=VMEM),
        cost_estimate=pl.CostEstimate(
            flops=8 * 2 * ROWS * WIDTH * 2 * HD, bytes_accessed=5 << 20, transcendentals=0
        ),
    )(where, *l_blocks, *d_blocks)


def finish_kernel(mine_ref, got_ref, k_ref, v_ref):
    total = mine_ref[...] + got_ref[...]
    k_ref[...] = total[:HD, :].T
    v_ref[...] = total[HD:, :].T


def finish(mine, got):
    return pl.pallas_call(
        finish_kernel,
        out_shape=(jax.ShapeDtypeStruct((WIDTH // 2, HD), f32),) * 2,
        compiler_params=pltpu.CompilerParams(vmem_limit_bytes=VMEM),
        cost_estimate=pl.CostEstimate(flops=WIDTH * HD, bytes_accessed=6 * WIDTH * HD, transcendentals=0),
    )(mine, got)


def first_visible(doc_lengths, block):
    order = jnp.arange(doc_lengths.shape[0], dtype=jnp.int32)
    ends = jnp.sum(jnp.where(order[:, None] <= order[None, :], doc_lengths[:, None], 0), axis=0)
    positions = block * ROWS + jnp.arange(ROWS, dtype=jnp.int32)
    first = jnp.max(jnp.where(ends[None, :] <= positions[:, None], ends[None, :], 0), axis=1)
    return jnp.broadcast_to(first[None, :].astype(jnp.int32), (8, ROWS))


def on_device(queries, key_states, value_states, attn_output, output_grad, log_norms, layer_input, doc_lengths):
    me = lax.axis_index("ctx").astype(jnp.int32)
    tp = lax.axis_index("tp").astype(jnp.int32)
    core, zl, y = me % 2, (me // 2) % 2, me // 4
    x, zh = tp // 2, tp % 2
    chip = me // 2

    kv = jnp.concatenate([key_states, value_states], axis=1)
    l_own = send(layer_input, spread)
    kv_got = [send(kv, within_half(flip, True)) for flip in (1, 2, 3)]

    aux_own = row_aux(output_grad, attn_output, log_norms)
    aux_par, q_par, do_par = (send(a, other_core) for a in (aux_own, queries, output_grad))
    first = (first_visible(doc_lengths, me), first_visible(doc_lengths, me ^ 1))
    aux, q, do = (aux_own, aux_par), (queries, q_par), (output_grad, do_par)

    l_other = send(l_own, shifted(dz=2))
    l_blocks = []
    for dx in (0, 1, 2, 3):
        for block in (l_own, l_other):
            l_blocks.append(block if dx == 0 else send(block, shifted(dx=-dx)))

    mine = jnp.stack([me, me, me ^ 1])
    dq_own, dq_par, dkv_own = attention(mine, kv, first, aux, q, do, None, (f32, f32), f32)
    far = jnp.stack([me ^ 2, me ^ 4, me ^ 6, me, me ^ 1])
    dq_own, dq_par, dkv_far = attention(
        far, jnp.concatenate(kv_got, axis=0), first, aux, q, do, (dq_own, dq_par), (f32, bf16), bf16
    )

    terms = [
        send(dkv_far[i * ROWS : (i + 1) * ROWS], within_half(flip, False)) for i, flip in enumerate((1, 2, 3))
    ]
    dq_got = send(dq_par, other_core)
    query_grad = ((dq_own + dq_got.astype(f32)) * SCALE).astype(bf16)

    dkv = dkv_own + terms[0].astype(f32) + terms[1].astype(f32) + terms[2].astype(f32)
    dkv = jnp.concatenate([dkv[:, :HD] * SCALE, dkv[:, HD:]], axis=1).astype(bf16)

    pair = jnp.concatenate([dkv, send(dkv, other_zl)], axis=0)
    d_blocks = [pair if dy == 0 else send(pair, shifted(dy=-dy)) for dy in (0, 1, 2, 3)]

    where = jnp.stack([(x + s - 2 * y) % 4 for s in range(4)] + [(zh ^ j) ^ zl for j in range(2)]).astype(jnp.int32)
    partial = weights(where, l_blocks, d_blocks)
    half = WIDTH // 2
    kept = lax.dynamic_slice(partial, (0, core * half), (2 * HD, half))
    sent = lax.dynamic_slice(partial, (0, (1 - core) * half), (2 * HD, half))
    key_weight, value_weight = finish(kept, send(sent, other_core))
    return query_grad, key_weight, value_weight


def solution(mesh):
    placed = (
        P("ctx", "tp"),
        P("ctx", "tp"),
        P("ctx", "tp"),
        P("ctx", "tp"),
        P("ctx", "tp"),
        P("tp", "ctx"),
        P("ctx", "tp"),
        P(),
    )
    return jax.shard_map(
        on_device,
        mesh=mesh,
        in_specs=placed,
        out_specs=(P("ctx", "tp"), P("ctx", "tp"), P("ctx", "tp")),
        check_vma=False,
    )
```

```python
import functools
import itertools
import math

import jax
import jax.numpy as jnp
from jax import lax
from jax.experimental import pallas as pl
from jax.experimental.pallas import tpu as pltpu
from jax.sharding import PartitionSpec as P

HD = 128
HEADS = 8
ROWS = 256
WIDTH = HEADS * HD
SCALE = 1.0 / math.sqrt(HD)
LOG2E = math.log2(math.e)
AXES = ("ctx", "tp")
DOCS = 16
STEP_HEADS = 4

f32 = jnp.float32
bf16 = jnp.bfloat16


def linear(x, y, z, core):
    zh, zl = divmod(z, 2)
    return ((y * 2 + zl) * 2 + core) * 8 + x * 2 + zh


def route(target):
    pairs = []
    for x, y, z, core in itertools.product(range(4), range(4), range(4), range(2)):
        to = target(x, y, z, core)
        if to is not None:
            pairs.append((linear(x, y, z, core), linear(*to)))
    return pairs


def send(value, target):
    return lax.ppermute(value, AXES, route(target))


def other_core(x, y, z, core):
    return (x, y, z, 1 - core)


def shifted(dx=0, dy=0, dz=0):
    return lambda x, y, z, core: ((x + dx) % 4, (y + dy) % 4, (z + dz) % 4, core)


def other_zl(x, y, z, core):
    return (x, y, z ^ 1, core)


def spread(x, y, z, core):
    zh, zl = divmod(z, 2)
    return ((x + y) % 4, x, zl * 2 + zh, core)


def within_half(flip, later):
    def target(x, y, z, core):
        place = (y % 2) * 2 + z % 2
        to = place ^ flip
        if (to > place) != later:
            return None
        return (x, y - y % 2 + to // 2, z - z % 2 + to % 2, core)

    return target


def nt(a, b):
    return lax.dot_general(a, b, (((1,), (1,)), ((), ())), preferred_element_type=f32)


def nn(a, b):
    return lax.dot_general(a, b, (((1,), (0,)), ((), ())), preferred_element_type=f32)


def tn(a, b):
    return lax.dot_general(a, b, (((0,), (0,)), ((), ())), preferred_element_type=f32)


def call(kernel, out_shape, operands, megabytes=12, flops=0, **more):
    return pl.pallas_call(
        kernel,
        out_shape=out_shape,
        compiler_params=pltpu.CompilerParams(vmem_limit_bytes=megabytes << 20),
        cost_estimate=pl.CostEstimate(flops=flops, bytes_accessed=1 << 16, transcendentals=0),
        **more,
    )(*operands)


def struct(shape, dtype):
    return jax.ShapeDtypeStruct(shape, dtype)


def join_kernel(k_ref, v_ref, kv_ref):
    kv_ref[:, :HD] = k_ref[...]
    kv_ref[:, HD:] = v_ref[...]


def aux_kernel(lengths_ref, do_ref, out_ref, ln_ref, aux_ref):
    for h in range(HEADS):
        cols = slice(h * HD, (h + 1) * HD)
        prod = do_ref[:, cols].astype(f32) * out_ref[:, cols].astype(f32)
        aux_ref[h : h + 1, :] = jnp.sum(prod.T, axis=0, keepdims=True)
    aux_ref[HEADS : 2 * HEADS, :] = ln_ref[...] * LOG2E
    positions = lax.axis_index("ctx") * ROWS + lax.broadcasted_iota(jnp.int32, (HEADS, ROWS), 1)
    end = jnp.int32(0)
    first = jnp.zeros((HEADS, ROWS), jnp.int32)
    for i in range(DOCS):
        end = end + lengths_ref[i]
        first = jnp.where(positions >= end, end, first)
    aux_ref[2 * HEADS :, :] = first.astype(f32)


def attention_kernel(flips, has_sum, *refs):
    refs = list(refs)
    take = lambda n: [refs.pop(0) for _ in range(n)]
    kv_refs, aux_refs, q_refs, do_refs = take(len(flips)), take(2), take(2), take(2)
    sums = take(2) if has_sum else None
    dq_refs = take(2)
    dkv_ref, dk_acc, dv_acc = refs
    step = pl.program_id(0)
    me = lax.axis_index("ctx")
    k = jnp.concatenate([r[:, :HD] for r in kv_refs], axis=0)
    v = jnp.concatenate([r[:, HD:] for r in kv_refs], axis=0)
    offset = lax.broadcasted_iota(jnp.int32, (ROWS, 1), 0)
    key_pos = jnp.concatenate([(me ^ flip) * ROWS + offset for flip in flips], axis=0)
    lane = lax.broadcasted_iota(jnp.int32, (1, ROWS), 1)
    dk = dv = None
    for i in range(2):
        query_pos = (me ^ i) * ROWS + lane
        first = aux_refs[i][2 * HEADS : 2 * HEADS + 1, :].astype(jnp.int32)
        visible = (key_pos <= query_pos) & (key_pos >= first)
        for j in range(STEP_HEADS):
            cols = slice(j * HD, (j + 1) * HD)
            h = step * STEP_HEADS + j
            q = q_refs[i][:, cols]
            do = do_refs[i][:, cols]
            dots = aux_refs[i][pl.ds(h, 1), :]
            norm = aux_refs[i][pl.ds(HEADS + h, 1), :]
            p = jnp.where(visible, jnp.exp2(nt(k, q) * (SCALE * LOG2E) - norm), 0.0)
            ds = (p * (nt(v, do) - dots)).astype(bf16)
            dv_term, dk_term, dq = nn(p.astype(bf16), do), nn(ds, q), tn(ds, k)
            dv = dv_term if dv is None else dv + dv_term
            dk = dk_term if dk is None else dk + dk_term
            if has_sum:
                dq = dq + sums[i][:, cols]
            dq_refs[i][:, cols] = dq.astype(dq_refs[i].dtype)

    @pl.when(step == 0)
    def _():
        dk_acc[...] = dk
        dv_acc[...] = dv

    @pl.when(step > 0)
    def _():
        dk_acc[...] += dk
        dv_acc[...] += dv

    @pl.when(step == pl.num_programs(0) - 1)
    def _():
        dkv_ref[:, :HD] = dk_acc[...].astype(dkv_ref.dtype)
        dkv_ref[:, HD:] = dv_acc[...].astype(dkv_ref.dtype)


def attention(flips, kv, aux, q, do, sums, dq_types, dkv_type):
    keys = len(flips) * ROWS
    whole = lambda a: pl.BlockSpec(a.shape, lambda s: (0,) * a.ndim)
    heads = pl.BlockSpec((ROWS, STEP_HEADS * HD), lambda s: (0, s))
    operands = [*kv, *aux, *q, *do, *(sums or ())]
    lead = len(kv) + len(aux)
    return call(
        functools.partial(attention_kernel, flips, sums is not None),
        (
            struct((ROWS, WIDTH), dq_types[0]),
            struct((ROWS, WIDTH), dq_types[1]),
            struct((keys, 2 * HD), dkv_type),
        ),
        operands,
        megabytes=24,
        grid=(HEADS // STEP_HEADS,),
        in_specs=[*map(whole, operands[:lead])] + [heads] * (len(operands) - lead),
        out_specs=[heads, heads, pl.BlockSpec((keys, 2 * HD), lambda s: (0, 0))],
        scratch_shapes=[pltpu.VMEM((keys, HD), f32)] * 2,
    )


def add_kernel(near_ref, got_ref, sum_ref, low_ref):
    total = near_ref[...] + got_ref[...].astype(f32)
    sum_ref[...] = total
    low_ref[...] = total.astype(bf16)


def close_kernel(sum_ref, got_ref, d_ref):
    for half in range(2):
        mine = slice(half * ROWS, (half + 1) * ROWS)
        its = slice((1 - half) * ROWS, (2 - half) * ROWS)
        total = sum_ref[mine, :] + got_ref[its, :].astype(f32)
        d_ref[half * 2 * HD : half * 2 * HD + HD, :] = (total[:, :HD] * SCALE).T.astype(bf16)
        d_ref[half * 2 * HD + HD : (half + 1) * 2 * HD, :] = total[:, HD:].T.astype(bf16)


def weights_kernel(where, *refs):
    l_refs, d_refs, (sent_ref, kept_ref, d_all) = refs[:8], refs[8:12], refs[12:]
    step = pl.program_id(0)

    @pl.when(step == 0)
    def _():
        for r in range(4):
            for half in range(2):
                d_all[r * 2 + half] = d_refs[r][half * 2 * HD : (half + 1) * 2 * HD, :]

    total = None
    for s in range(4):
        for j in range(2):
            term = nn(d_all[where[s] * 2 + where[4 + j]], l_refs[s * 2 + j][...])
            total = term if total is None else total + term

    @pl.when(step < pl.num_programs(0) // 2)
    def _():
        sent_ref[...] = total

    @pl.when(step >= pl.num_programs(0) // 2)
    def _():
        kept_ref[...] = total


def weights(where, l_blocks, d_blocks):
    tile, half = 256, 2
    return pl.pallas_call(
        weights_kernel,
        out_shape=(struct((2 * HD, WIDTH // 2), f32),) * 2,
        grid_spec=pltpu.PrefetchScalarGridSpec(
            num_scalar_prefetch=1,
            grid=(2 * half,),
            in_specs=[pl.BlockSpec((ROWS, tile), lambda s, w: (0, (s + half * (1 - w[6])) % (2 * half)))] * 8
            + [pl.BlockSpec((4 * HD, ROWS), lambda s, w: (0, 0))] * 4,
            out_specs=[
                pl.BlockSpec((2 * HD, tile), lambda s, w: (0, jnp.minimum(s, half - 1))),
                pl.BlockSpec((2 * HD, tile), lambda s, w: (0, jnp.maximum(s - half, 0))),
            ],
            scratch_shapes=[pltpu.VMEM((8, 2 * HD, ROWS), bf16)],
        ),
        compiler_params=pltpu.CompilerParams(vmem_limit_bytes=12 << 20),
        cost_estimate=pl.CostEstimate(flops=1 << 30, bytes_accessed=5 << 20, transcendentals=0),
    )(where, *l_blocks, *d_blocks)


def finish_kernel(mine_ref, got_ref, k_ref, v_ref):
    total = mine_ref[...] + got_ref[...]
    k_ref[...] = total[:HD, :].T
    v_ref[...] = total[HD:, :].T


def on_device(queries, key_states, value_states, attn_output, output_grad, log_norms, layer_input, doc_lengths):
    me = lax.axis_index("ctx").astype(jnp.int32)
    tp = lax.axis_index("tp").astype(jnp.int32)
    core, zl, y = me % 2, (me // 2) % 2, me // 4
    x, zh = tp // 2, tp % 2
    where = jnp.stack([(x + s - 2 * y) % 4 for s in range(4)] + [(zh ^ j) ^ zl for j in range(2)] + [core, core])

    kv = call(join_kernel, struct((ROWS, 2 * HD), bf16), (key_states, value_states))
    kv_zl, kv_y, kv_far = (send(kv, within_half(flip, True)) for flip in (1, 2, 3))
    l_own = send(layer_input, spread)

    aux_own = call(
        aux_kernel,
        struct((3 * HEADS, ROWS), f32),
        (doc_lengths, output_grad, attn_output, log_norms),
        in_specs=[pl.BlockSpec(memory_space=pltpu.SMEM)] + [pl.BlockSpec(memory_space=pltpu.VMEM)] * 3,
    )
    q_par, do_par, aux_par = (send(a, other_core) for a in (queries, output_grad, aux_own))
    aux, q, do = (aux_own, aux_par), (queries, q_par), (output_grad, do_par)

    l_other = send(l_own, shifted(dz=2))
    l_blocks = []
    for dx in (0, 1, 2, 3):
        for block in (l_own, l_other):
            l_blocks.append(block if dx == 0 else send(block, shifted(dx=-dx)))

    dq_own, dq_par, dkv_far = attention((4, 6), (kv_y, kv_far), aux, q, do, None, (f32, f32), bf16)
    got_far = send(dkv_far, within_half(2, False))
    dq_own, dq_par, dkv_near = attention((0, 2), (kv, kv_zl), aux, q, do, (dq_own, dq_par), (f32, bf16), f32)
    dq_got = send(dq_par, other_core)
    query_grad = ((dq_own + dq_got.astype(f32)) * SCALE).astype(bf16)

    pair = (2 * ROWS, 2 * HD)
    dkv, dkv_low = call(add_kernel, (struct(pair, f32), struct(pair, bf16)), (dkv_near, got_far))
    d_own = call(close_kernel, struct((4 * HD, ROWS), bf16), (dkv, send(dkv_low, other_zl)))
    d_blocks = [d_own if dy == 0 else send(d_own, shifted(dy=-dy)) for dy in (0, 1, 2, 3)]

    sent, kept = weights(where, l_blocks, d_blocks)
    key_weight, value_weight = call(
        finish_kernel, (struct((WIDTH // 2, HD), f32),) * 2, (kept, send(sent, other_core))
    )
    return query_grad, key_weight, value_weight


def solution(mesh):
    placed = (
        P("ctx", "tp"),
        P("ctx", "tp"),
        P("ctx", "tp"),
        P("ctx", "tp"),
        P("ctx", "tp"),
        P("tp", "ctx"),
        P("ctx", "tp"),
        P(),
    )
    return jax.shard_map(
        on_device,
        mesh=mesh,
        in_specs=placed,
        out_specs=(P("ctx", "tp"), P("ctx", "tp"), P("ctx", "tp")),
        check_vma=False,
    )
```

```python
import functools
import itertools
import math

import jax
import jax.numpy as jnp
from jax import lax
from jax.experimental import pallas as pl
from jax.experimental.pallas import tpu as pltpu
from jax.sharding import PartitionSpec as P

HD = 128
HEADS = 8
ROWS = 256
WIDTH = HEADS * HD
SCALE = 1.0 / math.sqrt(HD)
LOG2E = math.log2(math.e)
AXES = ("ctx", "tp")
DOCS = 16
STEP_HEADS = 4

f32 = jnp.float32
bf16 = jnp.bfloat16


def linear(x, y, z, core):
    zh, zl = divmod(z, 2)
    return ((y * 2 + zl) * 2 + core) * 8 + x * 2 + zh


def route(target):
    pairs = []
    for x, y, z, core in itertools.product(range(4), range(4), range(4), range(2)):
        to = target(x, y, z, core)
        if to is not None:
            pairs.append((linear(x, y, z, core), linear(*to)))
    return pairs


def send(value, target):
    return lax.ppermute(value, AXES, route(target))


def other_core(x, y, z, core):
    return (x, y, z, 1 - core)


def shifted(dx=0, dy=0, dz=0):
    return lambda x, y, z, core: ((x + dx) % 4, (y + dy) % 4, (z + dz) % 4, core)


def other_zl(x, y, z, core):
    return (x, y, z ^ 1, core)


def spread(x, y, z, core):
    zh, zl = divmod(z, 2)
    return ((x + y) % 4, x, zl * 2 + zh, core)


def within_half(flip, later):
    def target(x, y, z, core):
        place = (y % 2) * 2 + z % 2
        to = place ^ flip
        if (to > place) != later:
            return None
        return (x, y - y % 2 + to // 2, z - z % 2 + to % 2, core)

    return target


def nt(a, b):
    return lax.dot_general(a, b, (((1,), (1,)), ((), ())), preferred_element_type=f32)


def nn(a, b):
    return lax.dot_general(a, b, (((1,), (0,)), ((), ())), preferred_element_type=f32)


def tn(a, b):
    return lax.dot_general(a, b, (((0,), (0,)), ((), ())), preferred_element_type=f32)


def together(*arrays):
    return lax.optimization_barrier(arrays)


def call(kernel, out_shape, operands, megabytes=12, micros=0.01, **more):
    return pl.pallas_call(
        kernel,
        out_shape=out_shape,
        compiler_params=pltpu.CompilerParams(vmem_limit_bytes=megabytes << 20),
        cost_estimate=pl.CostEstimate(flops=int(micros * 1.15e9), bytes_accessed=1 << 16, transcendentals=0),
        **more,
    )(*operands)


def struct(shape, dtype):
    return jax.ShapeDtypeStruct(shape, dtype)


def prepare_kernel(lengths_ref, k_any, v_any, do_any, out_any, ln_any, kv_ref, aux_ref, do_ref, out_ref, sems):
    copies = [
        pltpu.make_async_copy(src, dst, sems.at[i])
        for i, (src, dst) in enumerate(
            (
                (k_any, kv_ref.at[:, :HD]),
                (v_any, kv_ref.at[:, HD:]),
                (ln_any, aux_ref.at[HEADS : 2 * HEADS, :]),
                (do_any, do_ref),
                (out_any, out_ref),
            )
        )
    ]
    for copy in copies:
        copy.start()
    positions = lax.axis_index("ctx") * ROWS + lax.broadcasted_iota(jnp.int32, (HEADS, ROWS), 1)
    end = jnp.int32(0)
    first = jnp.zeros((HEADS, ROWS), jnp.int32)
    for i in range(DOCS):
        end = end + lengths_ref[i]
        first = jnp.where(positions >= end, end, first)
    aux_ref[2 * HEADS :, :] = first.astype(f32)
    for copy in copies:
        copy.wait()
    aux_ref[HEADS : 2 * HEADS, :] = aux_ref[HEADS : 2 * HEADS, :] * LOG2E
    for h in range(HEADS):
        cols = slice(h * HD, (h + 1) * HD)
        prod = do_ref[:, cols].astype(f32) * out_ref[:, cols].astype(f32)
        aux_ref[h : h + 1, :] = jnp.sum(prod.T, axis=0, keepdims=True)


def prepare(doc_lengths, k, v, do, out, ln):
    return call(
        prepare_kernel,
        (struct((ROWS, 2 * HD), bf16), struct((3 * HEADS, ROWS), f32)),
        (doc_lengths, k, v, do, out, ln),
        in_specs=[pl.BlockSpec(memory_space=pltpu.SMEM)] + [pl.BlockSpec(memory_space=pltpu.HBM)] * 5,
        megabytes=60,
        micros=0.3,
        scratch_shapes=[pltpu.VMEM((ROWS, WIDTH), bf16)] * 2 + [pltpu.SemaphoreType.DMA((5,))],
    )


def attention_kernel(flips, has_sum, *refs):
    refs = list(refs)
    take = lambda n: [refs.pop(0) for _ in range(n)]
    kv_refs, aux_refs, q_refs, do_refs = take(len(flips)), take(2), take(2), take(2)
    sums = take(2) if has_sum else None
    dq_refs = take(2)
    dkv_ref, dk_acc, dv_acc = refs
    me = lax.axis_index("ctx")
    dk_acc[...] = jnp.zeros_like(dk_acc)
    dv_acc[...] = jnp.zeros_like(dv_acc)

    @pl.loop(0, HEADS // STEP_HEADS)
    def _(step):
        k = jnp.concatenate([r[:, :HD] for r in kv_refs], axis=0)
        v = jnp.concatenate([r[:, HD:] for r in kv_refs], axis=0)
        offset = lax.broadcasted_iota(jnp.int32, (ROWS, 1), 0)
        key_pos = jnp.concatenate([(me ^ flip) * ROWS + offset for flip in flips], axis=0)
        lane = lax.broadcasted_iota(jnp.int32, (1, ROWS), 1)
        dk = dv = None
        for i in range(2):
            query_pos = (me ^ i) * ROWS + lane
            first = aux_refs[i][2 * HEADS : 2 * HEADS + 1, :].astype(jnp.int32)
            visible = (key_pos <= query_pos) & (key_pos >= first)
            for j in range(STEP_HEADS):
                h = step * STEP_HEADS + j
                cols = pl.ds(pl.multiple_of(h * HD, HD), HD)
                q = q_refs[i][:, cols]
                do = do_refs[i][:, cols]
                dots = aux_refs[i][pl.ds(h, 1), :]
                norm = aux_refs[i][pl.ds(HEADS + h, 1), :]
                p = jnp.where(visible, jnp.exp2(nt(k, q) * (SCALE * LOG2E) - norm), 0.0)
                ds = (p * (nt(v, do) - dots)).astype(bf16)
                dv_term, dk_term, dq = nn(p.astype(bf16), do), nn(ds, q), tn(ds, k)
                dv = dv_term if dv is None else dv + dv_term
                dk = dk_term if dk is None else dk + dk_term
                if has_sum:
                    dq = dq + sums[i][:, cols]
                dq_refs[i][:, cols] = dq.astype(dq_refs[i].dtype)
        dk_acc[...] += dk
        dv_acc[...] += dv

    dkv_ref[:, :HD] = dk_acc[...].astype(dkv_ref.dtype)
    dkv_ref[:, HD:] = dv_acc[...].astype(dkv_ref.dtype)


def attention(flips, kv, aux, q, do, sums, dq_types, dkv_type, micros):
    keys = len(flips) * ROWS
    return call(
        functools.partial(attention_kernel, flips, sums is not None),
        (
            struct((ROWS, WIDTH), dq_types[0]),
            struct((ROWS, WIDTH), dq_types[1]),
            struct((keys, 2 * HD), dkv_type),
        ),
        [*kv, *aux, *q, *do, *(sums or ())],
        megabytes=24,
        micros=micros,
        scratch_shapes=[pltpu.VMEM((keys, HD), f32)] * 2,
    )


def add_kernel(own_ref, zl_ref, got_ref, sum_ref, low_ref):
    for half, near_ref in enumerate((own_ref, zl_ref)):
        rows = slice(half * ROWS, (half + 1) * ROWS)
        total = near_ref[...] + got_ref[rows, :].astype(f32)
        sum_ref[rows, :] = total
        low_ref[rows, :] = total.astype(bf16)


def close_kernel(sum_ref, got_ref, d_ref):
    for half in range(2):
        mine = slice(half * ROWS, (half + 1) * ROWS)
        its = slice((1 - half) * ROWS, (2 - half) * ROWS)
        total = sum_ref[mine, :] + got_ref[its, :].astype(f32)
        d_ref[half * 2 * HD : half * 2 * HD + HD, :] = (total[:, :HD] * SCALE).T.astype(bf16)
        d_ref[half * 2 * HD + HD : (half + 1) * 2 * HD, :] = total[:, HD:].T.astype(bf16)


def weights_kernel(*refs):
    l_refs, d_refs, (sent_ref, kept_ref, d_all) = refs[:8], refs[8:12], refs[12:]
    me, tp = lax.axis_index("ctx"), lax.axis_index("tp")
    core, zl, y = me % 2, (me // 2) % 2, me // 4
    x, zh = tp // 2, tp % 2
    for r in range(4):
        for half in range(2):
            d_all[r * 2 + half] = d_refs[r][half * 2 * HD : (half + 1) * 2 * HD, :]
    half_width = WIDTH // 2
    for out_ref, whose in ((sent_ref, 1 - core), (kept_ref, core)):
        for t in range(2):
            tile = half_width // 2
            cols = pl.ds(pl.multiple_of(whose * half_width + t * tile, tile), tile)
            total = None
            for s in range(4):
                for j in range(2):
                    slot = ((x + s + 2 * y) % 4) * 2 + ((zh ^ j) ^ zl)
                    term = nn(d_all[slot], l_refs[s * 2 + j][:, cols])
                    total = term if total is None else total + term
            out_ref[:, t * tile : (t + 1) * tile] = total


def weights(l_blocks, d_blocks):
    return call(
        weights_kernel,
        (struct((2 * HD, WIDTH // 2), f32),) * 2,
        (*l_blocks, *d_blocks),
        scratch_shapes=[pltpu.VMEM((8, 2 * HD, ROWS), bf16)],
    )


def finish_kernel(mine_ref, got_ref, k_ref, v_ref):
    total = mine_ref[...] + got_ref[...]
    k_ref[...] = total[:HD, :].T
    v_ref[...] = total[HD:, :].T


def on_device(queries, key_states, value_states, attn_output, output_grad, log_norms, layer_input, doc_lengths):
    q_par, do_par = (send(a, other_core) for a in (queries, output_grad))
    l_own = send(layer_input, spread)
    kv, aux_own = prepare(doc_lengths, key_states, value_states, output_grad, attn_output, log_norms)
    kv, aux_own, q_par, do_par = together(kv, aux_own, q_par, do_par)
    aux_par = send(aux_own, other_core)
    aux, q, do = (aux_own, aux_par), (queries, q_par), (output_grad, do_par)

    kv_far, kv_y, kv_zl = (send(kv, within_half(flip, True)) for flip in (3, 2, 1))

    behind, ahead, across = shifted(dx=-1), shifted(dx=1), shifted(dz=2)
    *dqs, dkv_own = attention((0,), (kv,), aux, q, do, None, (f32, f32), f32, 0.3)
    l_own, dkv_own, kv_y, kv_far, *dqs = together(l_own, dkv_own, kv_y, kv_far, *dqs)
    own_1, own_3, other_0 = send(l_own, behind), send(l_own, ahead), send(l_own, across)

    *dqs, dkv_far = attention((4, 6), (kv_y, kv_far), aux, q, do, dqs, (f32, f32), bf16, 0.3)
    got_far = send(dkv_far, within_half(2, False))
    dq_own, dq_par, dkv_zl = attention((2,), (kv_zl,), aux, q, do, dqs, (f32, bf16), f32, 1.5)
    dq_own, dq_par, dkv_zl, got_far, own_1, own_3, other_0 = together(
        dq_own, dq_par, dkv_zl, got_far, own_1, own_3, other_0
    )
    own_2, other_3 = send(own_1, behind), send(other_0, ahead)

    dq_got = send(dq_par, other_core)
    query_grad = ((dq_own + dq_got.astype(f32)) * SCALE).astype(bf16)

    pair = (2 * ROWS, 2 * HD)
    dkv, dkv_low = call(add_kernel, (struct(pair, f32), struct(pair, bf16)), (dkv_own, dkv_zl, got_far))
    got_zl = send(dkv_low, other_zl)
    got_zl, query_grad = together(got_zl, query_grad)
    d_own = call(close_kernel, struct((4 * HD, ROWS), bf16), (dkv, got_zl))
    own_2, other_3, other_0, _ = together(own_2, other_3, other_0, d_own)
    other_1, other_2 = send(other_0, behind), send(own_2, across)
    d_blocks = (d_own, *(send(d_own, shifted(dy=-dy)) for dy in (1, 2, 3)))

    l_blocks = (l_own, other_0, own_1, other_1, own_2, other_2, own_3, other_3)
    sent, kept = weights(l_blocks, d_blocks)
    key_weight, value_weight = call(
        finish_kernel, (struct((WIDTH // 2, HD), f32),) * 2, (kept, send(sent, other_core))
    )
    return query_grad, key_weight, value_weight


def solution(mesh):
    placed = (
        P("ctx", "tp"),
        P("ctx", "tp"),
        P("ctx", "tp"),
        P("ctx", "tp"),
        P("ctx", "tp"),
        P("tp", "ctx"),
        P("ctx", "tp"),
        P(),
    )
    return jax.shard_map(
        on_device,
        mesh=mesh,
        in_specs=placed,
        out_specs=(P("ctx", "tp"), P("ctx", "tp"), P("ctx", "tp")),
        check_vma=False,
    )
```

```python
import functools
import itertools
import math

import jax
import jax.numpy as jnp
from jax import lax
from jax.experimental import pallas as pl
from jax.experimental.pallas import tpu as pltpu
from jax.sharding import PartitionSpec as P

HD = 128
HEADS = 8
ROWS = 256
WIDTH = HEADS * HD
SCALE = 1.0 / math.sqrt(HD)
LOG2E = math.log2(math.e)
AXES = ("ctx", "tp")
DOCS = 16
STEP_HEADS = 4

f32 = jnp.float32
bf16 = jnp.bfloat16


def linear(x, y, z, core):
    zh, zl = divmod(z, 2)
    return ((y * 2 + zl) * 2 + core) * 8 + x * 2 + zh


def route(target):
    pairs = []
    for x, y, z, core in itertools.product(range(4), range(4), range(4), range(2)):
        to = target(x, y, z, core)
        if to is not None:
            pairs.append((linear(x, y, z, core), linear(*to)))
    return pairs


def send(value, target):
    return lax.ppermute(value, AXES, route(target))


def other_core(x, y, z, core):
    return (x, y, z, 1 - core)


def shifted(dx=0, dy=0, dz=0):
    return lambda x, y, z, core: ((x + dx) % 4, (y + dy) % 4, (z + dz) % 4, core)


def other_zl(x, y, z, core):
    return (x, y, z ^ 1, core)


def spread(x, y, z, core):
    zh, zl = divmod(z, 2)
    return ((x + y) % 4, x, zl * 2 + zh, core)


def within_half(flip, later):
    def target(x, y, z, core):
        place = (y % 2) * 2 + z % 2
        to = place ^ flip
        if (to > place) != later:
            return None
        return (x, y - y % 2 + to // 2, z - z % 2 + to % 2, core)

    return target


def nt(a, b):
    return lax.dot_general(a, b, (((1,), (1,)), ((), ())), preferred_element_type=f32)


def nn(a, b):
    return lax.dot_general(a, b, (((1,), (0,)), ((), ())), preferred_element_type=f32)


def tn(a, b):
    return lax.dot_general(a, b, (((0,), (0,)), ((), ())), preferred_element_type=f32)


def together(*arrays):
    return lax.optimization_barrier(arrays)


def call(kernel, out_shape, operands, megabytes=12, micros=0.01, **more):
    return pl.pallas_call(
        kernel,
        out_shape=out_shape,
        compiler_params=pltpu.CompilerParams(vmem_limit_bytes=megabytes << 20),
        cost_estimate=pl.CostEstimate(flops=int(micros * 1.15e9), bytes_accessed=1 << 16, transcendentals=0),
        **more,
    )(*operands)


def struct(shape, dtype):
    return jax.ShapeDtypeStruct(shape, dtype)


def arrived_kernel(*refs):
    refs[-1][...] = jnp.zeros_like(refs[-1])


def arrived(arrays, micros):
    return call(
        arrived_kernel,
        struct((8, 128), f32),
        arrays,
        micros=micros,
        in_specs=[pl.BlockSpec(memory_space=pl.ANY)] * len(arrays),
    )


def prepare_kernel(lengths_ref, k_any, v_any, do_any, out_any, ln_any, kv_ref, aux_ref, do_ref, out_ref, sems):
    copies = [
        pltpu.make_async_copy(src, dst, sems.at[i])
        for i, (src, dst) in enumerate(
            (
                (k_any, kv_ref.at[:, :HD]),
                (v_any, kv_ref.at[:, HD:]),
                (ln_any, aux_ref.at[HEADS : 2 * HEADS, :]),
                (do_any, do_ref),
                (out_any, out_ref),
            )
        )
    ]
    for copy in copies:
        copy.start()
    positions = lax.axis_index("ctx") * ROWS + lax.broadcasted_iota(jnp.int32, (HEADS, ROWS), 1)
    end = jnp.int32(0)
    first = jnp.zeros((HEADS, ROWS), jnp.int32)
    for i in range(DOCS):
        end = end + lengths_ref[i]
        first = jnp.where(positions >= end, end, first)
    aux_ref[2 * HEADS :, :] = first.astype(f32)
    for copy in copies:
        copy.wait()
    aux_ref[HEADS : 2 * HEADS, :] = aux_ref[HEADS : 2 * HEADS, :] * LOG2E
    for h in range(HEADS):
        cols = slice(h * HD, (h + 1) * HD)
        prod = do_ref[:, cols].astype(f32) * out_ref[:, cols].astype(f32)
        aux_ref[h : h + 1, :] = jnp.sum(prod.T, axis=0, keepdims=True)


def prepare(doc_lengths, k, v, do, out, ln):
    return call(
        prepare_kernel,
        (struct((ROWS, 2 * HD), bf16), struct((3 * HEADS, ROWS), f32)),
        (doc_lengths, k, v, do, out, ln),
        in_specs=[pl.BlockSpec(memory_space=pltpu.SMEM)] + [pl.BlockSpec(memory_space=pltpu.HBM)] * 5,
        megabytes=56,
        micros=0.3,
        scratch_shapes=[pltpu.VMEM((ROWS, WIDTH), bf16)] * 2 + [pltpu.SemaphoreType.DMA((5,))],
    )


def attention_kernel(flips, has_sum, *refs):
    refs = list(refs)
    take = lambda n: [refs.pop(0) for _ in range(n)]
    kv_refs, aux_refs, q_refs, do_refs = take(len(flips)), take(2), take(2), take(2)
    sums = take(2) if has_sum else None
    dq_refs = take(2)
    dkv_ref, dk_acc, dv_acc = refs
    me = lax.axis_index("ctx")
    dk_acc[...] = jnp.zeros_like(dk_acc)
    dv_acc[...] = jnp.zeros_like(dv_acc)

    @pl.loop(0, HEADS // STEP_HEADS)
    def _(step):
        k = jnp.concatenate([r[:, :HD] for r in kv_refs], axis=0)
        v = jnp.concatenate([r[:, HD:] for r in kv_refs], axis=0)
        offset = lax.broadcasted_iota(jnp.int32, (ROWS, 1), 0)
        key_pos = jnp.concatenate([(me ^ flip) * ROWS + offset for flip in flips], axis=0)
        lane = lax.broadcasted_iota(jnp.int32, (1, ROWS), 1)
        dk = dv = None
        for i in range(2):
            query_pos = (me ^ i) * ROWS + lane
            first = aux_refs[i][2 * HEADS : 2 * HEADS + 1, :].astype(jnp.int32)
            visible = (key_pos <= query_pos) & (key_pos >= first)
            for j in range(STEP_HEADS):
                h = step * STEP_HEADS + j
                cols = pl.ds(pl.multiple_of(h * HD, HD), HD)
                q = q_refs[i][:, cols]
                do = do_refs[i][:, cols]
                dots = aux_refs[i][pl.ds(h, 1), :]
                norm = aux_refs[i][pl.ds(HEADS + h, 1), :]
                p = jnp.where(visible, jnp.exp2(nt(k, q) * (SCALE * LOG2E) - norm), 0.0)
                ds = (p * (nt(v, do) - dots)).astype(bf16)
                dv_term, dk_term, dq = nn(p.astype(bf16), do), nn(ds, q), tn(ds, k)
                dv = dv_term if dv is None else dv + dv_term
                dk = dk_term if dk is None else dk + dk_term
                if has_sum:
                    dq = dq + sums[i][:, cols]
                dq_refs[i][:, cols] = dq.astype(dq_refs[i].dtype)
        dk_acc[...] += dk
        dv_acc[...] += dv

    dkv_ref[:, :HD] = dk_acc[...].astype(dkv_ref.dtype)
    dkv_ref[:, HD:] = dv_acc[...].astype(dkv_ref.dtype)


def attention(flips, kv, aux, q, do, sums, dq_types, dkv_type, micros):
    keys = len(flips) * ROWS
    return call(
        functools.partial(attention_kernel, flips, sums is not None),
        (
            struct((ROWS, WIDTH), dq_types[0]),
            struct((ROWS, WIDTH), dq_types[1]),
            struct((keys, 2 * HD), dkv_type),
        ),
        [*kv, *aux, *q, *do, *(sums or ())],
        megabytes=24,
        micros=micros,
        scratch_shapes=[pltpu.VMEM((keys, HD), f32)] * 2,
    )


def add_kernel(own_ref, zl_ref, got_ref, sum_ref, low_ref):
    for half, near_ref in enumerate((own_ref, zl_ref)):
        rows = slice(half * ROWS, (half + 1) * ROWS)
        total = near_ref[...] + got_ref[rows, :].astype(f32)
        sum_ref[rows, :] = total
        low_ref[rows, :] = total.astype(bf16)


def close_kernel(sum_ref, got_ref, d_ref):
    for half in range(2):
        mine = slice(half * ROWS, (half + 1) * ROWS)
        its = slice((1 - half) * ROWS, (2 - half) * ROWS)
        total = sum_ref[mine, :] + got_ref[its, :].astype(f32)
        k_grad = (total[:, :HD] * SCALE).T.astype(bf16)
        v_grad = total[:, HD:].T.astype(bf16)
        for copy in range(4):
            d_ref[copy, half * 2 * HD : half * 2 * HD + HD, :] = k_grad
            d_ref[copy, half * 2 * HD + HD : (half + 1) * 2 * HD, :] = v_grad


def weights_kernel(*refs):
    l_refs, (d_ref, _, sent_ref, kept_ref) = refs[:8], refs[8:]
    me, tp = lax.axis_index("ctx"), lax.axis_index("tp")
    core, zl, y = me % 2, (me // 2) % 2, me // 4
    x, zh = tp // 2, tp % 2
    half_width = WIDTH // 2
    for out_ref, whose in ((sent_ref, 1 - core), (kept_ref, core)):
        for t in range(2):
            tile = half_width // 2
            cols = pl.ds(pl.multiple_of(whose * half_width + t * tile, tile), tile)
            total = None
            for s in range(4):
                for j in range(2):
                    rows = pl.ds(pl.multiple_of(((zh ^ j) ^ zl) * 2 * HD, 2 * HD), 2 * HD)
                    term = nn(d_ref[(x + s + 3 * y) % 4, rows, :], l_refs[s * 2 + j][:, cols])
                    total = term if total is None else total + term
            out_ref[:, t * tile : (t + 1) * tile] = total


def weights(l_blocks, d_blocks, ready):
    return call(
        weights_kernel,
        (struct((2 * HD, WIDTH // 2), f32),) * 2,
        (*l_blocks, d_blocks, ready),
    )


def finish_kernel(mine_ref, got_ref, k_ref, v_ref):
    total = mine_ref[...] + got_ref[...]
    k_ref[...] = total[:HD, :].T
    v_ref[...] = total[HD:, :].T


def on_device(queries, key_states, value_states, attn_output, output_grad, log_norms, layer_input, doc_lengths):
    q_par, do_par = (send(a, other_core) for a in (queries, output_grad))
    l_own = send(layer_input, spread)
    kv, aux_own = prepare(doc_lengths, key_states, value_states, output_grad, attn_output, log_norms)
    kv, aux_own, q_par, do_par = together(kv, aux_own, q_par, do_par)
    aux_par = send(aux_own, other_core)
    aux, q, do = (aux_own, aux_par), (queries, q_par), (output_grad, do_par)

    kv_far, kv_y, kv_zl = (send(kv, within_half(flip, True)) for flip in (3, 2, 1))

    behind, ahead, across = shifted(dx=-1), shifted(dx=1), shifted(dz=2)
    *dqs, dkv_own = attention((0,), (kv,), aux, q, do, None, (f32, f32), f32, 0.3)
    l_own, dkv_own, kv_y, kv_far, kv_zl, *dqs = together(l_own, dkv_own, kv_y, kv_far, kv_zl, *dqs)
    own_1, own_3, other_0 = (send(l_own, t) for t in (behind, ahead, across))

    *dqs, dkv_far = attention((4, 6), (kv_y, kv_far), aux, q, do, dqs, (f32, f32), bf16, 0.3)
    got_far = send(dkv_far, within_half(2, False))
    dq_own, dq_par, dkv_zl = attention((2,), (kv_zl,), aux, q, do, dqs, (f32, bf16), f32, 1.5)
    dq_own, dq_par, dkv_zl, got_far, l_own, own_1, own_3, other_0 = together(
        dq_own, dq_par, dkv_zl, got_far, l_own, own_1, own_3, other_0
    )
    dq_got = send(dq_par, other_core)
    query_grad = ((dq_own + dq_got.astype(f32)) * SCALE).astype(bf16)

    pair = (2 * ROWS, 2 * HD)
    dkv, dkv_low = call(add_kernel, (struct(pair, f32), struct(pair, bf16)), (dkv_own, dkv_zl, got_far))
    got_zl = send(dkv_low, other_zl)
    other_0, own_1, _ = together(other_0, own_1, dkv_low)
    other_3, own_2, other_1 = send(other_0, ahead), send(own_1, behind), send(other_0, behind)
    got_zl, query_grad, other_3 = together(got_zl, query_grad, other_3)
    d_copies = call(close_kernel, struct((4, 4 * HD, ROWS), bf16), (dkv, got_zl))
    columns = [[y * 4 + rest for y in range(4)] for rest in range(4)]
    d_blocks = lax.all_to_all(d_copies, "ctx", 0, 0, axis_index_groups=columns)

    other_2 = send(other_3, ahead)
    ready = arrived((own_2, other_1, other_2), 8)
    l_blocks = (l_own, other_0, own_1, other_1, own_2, other_2, own_3, other_3)
    sent, kept = weights(l_blocks, d_blocks, ready)
    key_weight, value_weight = call(
        finish_kernel, (struct((WIDTH // 2, HD), f32),) * 2, (kept, send(sent, other_core))
    )
    return query_grad, key_weight, value_weight


def solution(mesh):
    placed = (
        P("ctx", "tp"),
        P("ctx", "tp"),
        P("ctx", "tp"),
        P("ctx", "tp"),
        P("ctx", "tp"),
        P("tp", "ctx"),
        P("ctx", "tp"),
        P(),
    )
    return jax.shard_map(
        on_device,
        mesh=mesh,
        in_specs=placed,
        out_specs=(P("ctx", "tp"), P("ctx", "tp"), P("ctx", "tp")),
        check_vma=False,
    )
```

```python
import functools
import itertools
import math

import jax
import jax.numpy as jnp
from jax import lax
from jax.experimental import pallas as pl
from jax.experimental.pallas import tpu as pltpu
from jax.sharding import PartitionSpec as P

HD = 128
HEADS = 8
ROWS = 256
WIDTH = HEADS * HD
SCALE = 1.0 / math.sqrt(HD)
LOG2E = math.log2(math.e)
AXES = ("ctx", "tp")
DOCS = 16
STEP_HEADS = 4

f32 = jnp.float32
bf16 = jnp.bfloat16


def linear(x, y, z, core):
    zh, zl = divmod(z, 2)
    return ((y * 2 + zl) * 2 + core) * 8 + x * 2 + zh


def route(target):
    pairs = []
    for x, y, z, core in itertools.product(range(4), range(4), range(4), range(2)):
        to = target(x, y, z, core)
        if to is not None:
            pairs.append((linear(x, y, z, core), linear(*to)))
    return pairs


def send(value, target):
    return lax.ppermute(value, AXES, route(target))


def other_core(x, y, z, core):
    return (x, y, z, 1 - core)


def shifted(dx=0, dy=0, dz=0):
    return lambda x, y, z, core: ((x + dx) % 4, (y + dy) % 4, (z + dz) % 4, core)


def other_zl(x, y, z, core):
    return (x, y, z ^ 1, core)


def spread(x, y, z, core):
    zh, zl = divmod(z, 2)
    return ((x + y) % 4, x, zl * 2 + zh, core)


def within_half(flip, later):
    def target(x, y, z, core):
        place = (y % 2) * 2 + z % 2
        to = place ^ flip
        if (to > place) != later:
            return None
        return (x, y - y % 2 + to // 2, z - z % 2 + to % 2, core)

    return target


def nt(a, b):
    return lax.dot_general(a, b, (((1,), (1,)), ((), ())), preferred_element_type=f32)


def nn(a, b):
    return lax.dot_general(a, b, (((1,), (0,)), ((), ())), preferred_element_type=f32)


def tn(a, b):
    return lax.dot_general(a, b, (((0,), (0,)), ((), ())), preferred_element_type=f32)


def together(*arrays):
    return lax.optimization_barrier(arrays)


def call(kernel, out_shape, operands, megabytes=12, micros=0.01, **more):
    return pl.pallas_call(
        kernel,
        out_shape=out_shape,
        compiler_params=pltpu.CompilerParams(vmem_limit_bytes=megabytes << 20),
        cost_estimate=pl.CostEstimate(flops=int(micros * 1.15e9), bytes_accessed=1 << 16, transcendentals=0),
        **more,
    )(*operands)


def struct(shape, dtype):
    return jax.ShapeDtypeStruct(shape, dtype)


def arrived_kernel(*refs):
    refs[-1][...] = jnp.zeros_like(refs[-1])


def arrived(arrays, micros):
    return call(
        arrived_kernel,
        struct((8, 128), f32),
        arrays,
        micros=micros,
        in_specs=[pl.BlockSpec(memory_space=pl.ANY)] * len(arrays),
    )


def prepare_kernel(lengths_ref, k_any, v_any, do_any, out_any, ln_any, kv_ref, aux_ref, do_ref, out_ref, sems):
    copies = [
        pltpu.make_async_copy(src, dst, sems.at[i])
        for i, (src, dst) in enumerate(
            (
                (k_any, kv_ref.at[:, :HD]),
                (v_any, kv_ref.at[:, HD:]),
                (ln_any, aux_ref.at[HEADS : 2 * HEADS, :]),
                (do_any, do_ref),
                (out_any, out_ref),
            )
        )
    ]
    for copy in copies:
        copy.start()
    positions = lax.axis_index("ctx") * ROWS + lax.broadcasted_iota(jnp.int32, (HEADS, ROWS), 1)
    end = jnp.int32(0)
    first = jnp.zeros((HEADS, ROWS), jnp.int32)
    for i in range(DOCS):
        end = end + lengths_ref[i]
        first = jnp.where(positions >= end, end, first)
    aux_ref[2 * HEADS :, :] = first.astype(f32)
    for copy in copies:
        copy.wait()
    aux_ref[HEADS : 2 * HEADS, :] = aux_ref[HEADS : 2 * HEADS, :] * LOG2E
    for h in range(HEADS):
        cols = slice(h * HD, (h + 1) * HD)
        prod = do_ref[:, cols].astype(f32) * out_ref[:, cols].astype(f32)
        aux_ref[h : h + 1, :] = jnp.sum(prod.T, axis=0, keepdims=True)


def prepare(doc_lengths, k, v, do, out, ln):
    return call(
        prepare_kernel,
        (struct((ROWS, 2 * HD), bf16), struct((3 * HEADS, ROWS), f32)),
        (doc_lengths, k, v, do, out, ln),
        in_specs=[pl.BlockSpec(memory_space=pltpu.SMEM)] + [pl.BlockSpec(memory_space=pltpu.HBM)] * 5,
        megabytes=56,
        micros=0.3,
        scratch_shapes=[pltpu.VMEM((ROWS, WIDTH), bf16)] * 2 + [pltpu.SemaphoreType.DMA((5,))],
    )


def attention_kernel(flips, has_sum, *refs):
    refs = list(refs)
    take = lambda n: [refs.pop(0) for _ in range(n)]
    kv_refs, aux_refs, q_refs, do_refs = take(len(flips)), take(2), take(2), take(2)
    sums = take(2) if has_sum else None
    dq_refs = take(2)
    dkv_ref, dk_acc, dv_acc = refs
    me = lax.axis_index("ctx")
    dk_acc[...] = jnp.zeros_like(dk_acc)
    dv_acc[...] = jnp.zeros_like(dv_acc)

    @pl.loop(0, HEADS // STEP_HEADS)
    def _(step):
        k = jnp.concatenate([r[:, :HD] for r in kv_refs], axis=0)
        v = jnp.concatenate([r[:, HD:] for r in kv_refs], axis=0)
        offset = lax.broadcasted_iota(jnp.int32, (ROWS, 1), 0)
        key_pos = jnp.concatenate([(me ^ flip) * ROWS + offset for flip in flips], axis=0)
        lane = lax.broadcasted_iota(jnp.int32, (1, ROWS), 1)
        dk = dv = None
        for i in range(2):
            query_pos = (me ^ i) * ROWS + lane
            first = aux_refs[i][2 * HEADS : 2 * HEADS + 1, :].astype(jnp.int32)
            visible = (key_pos <= query_pos) & (key_pos >= first)
            for j in range(STEP_HEADS):
                h = step * STEP_HEADS + j
                cols = pl.ds(pl.multiple_of(h * HD, HD), HD)
                q = q_refs[i][:, cols]
                do = do_refs[i][:, cols]
                dots = aux_refs[i][pl.ds(h, 1), :]
                norm = aux_refs[i][pl.ds(HEADS + h, 1), :]
                p = jnp.where(visible, jnp.exp2(nt(k, q) * (SCALE * LOG2E) - norm), 0.0)
                ds = (p * (nt(v, do) - dots)).astype(bf16)
                dv_term, dk_term, dq = nn(p.astype(bf16), do), nn(ds, q), tn(ds, k)
                dv = dv_term if dv is None else dv + dv_term
                dk = dk_term if dk is None else dk + dk_term
                if has_sum:
                    dq = dq + sums[i][:, cols]
                dq_refs[i][:, cols] = dq.astype(dq_refs[i].dtype)
        dk_acc[...] += dk
        dv_acc[...] += dv

    dkv_ref[:, :HD] = dk_acc[...].astype(dkv_ref.dtype)
    dkv_ref[:, HD:] = dv_acc[...].astype(dkv_ref.dtype)


def attention(flips, kv, aux, q, do, sums, dq_types, dkv_type, micros):
    keys = len(flips) * ROWS
    return call(
        functools.partial(attention_kernel, flips, sums is not None),
        (
            struct((ROWS, WIDTH), dq_types[0]),
            struct((ROWS, WIDTH), dq_types[1]),
            struct((keys, 2 * HD), dkv_type),
        ),
        [*kv, *aux, *q, *do, *(sums or ())],
        megabytes=14,
        micros=micros,
        scratch_shapes=[pltpu.VMEM((keys, HD), f32)] * 2,
    )


def add_kernel(own_ref, zl_ref, got_ref, sum_ref, low_ref):
    for half, near_ref in enumerate((own_ref, zl_ref)):
        rows = slice(half * ROWS, (half + 1) * ROWS)
        total = near_ref[...] + got_ref[rows, :].astype(f32)
        sum_ref[rows, :] = total
        low_ref[rows, :] = total.astype(bf16)


def close_kernel(sum_ref, got_ref, d_ref):
    for half in range(2):
        mine = slice(half * ROWS, (half + 1) * ROWS)
        its = slice((1 - half) * ROWS, (2 - half) * ROWS)
        total = sum_ref[mine, :] + got_ref[its, :].astype(f32)
        k_grad = (total[:, :HD] * SCALE).T.astype(bf16)
        v_grad = total[:, HD:].T.astype(bf16)
        for copy in range(4):
            d_ref[copy, half * 2 * HD : half * 2 * HD + HD, :] = k_grad
            d_ref[copy, half * 2 * HD + HD : (half + 1) * 2 * HD, :] = v_grad


def weights_kernel(own_half, *refs):
    l_refs, (d_ref, _, out_ref, held, sems) = refs[:8], refs[8:]
    me, tp = lax.axis_index("ctx"), lax.axis_index("tp")
    core, zl, y = me % 2, (me // 2) % 2, me // 4
    x, zh = tp // 2, tp % 2
    half_width = WIDTH // 2
    whose = core if own_half else 1 - core
    cols = pl.ds(pl.multiple_of(whose * half_width, half_width), half_width)
    copies = [pltpu.make_async_copy(ref.at[:, cols], held.at[i], sems.at[i]) for i, ref in enumerate(l_refs)]
    for copy in copies:
        copy.start()
    for s in range(4):
        for j in range(2):
            i = s * 2 + j
            rows = pl.ds(pl.multiple_of(((zh ^ j) ^ zl) * 2 * HD, 2 * HD), 2 * HD)
            copies[i].wait()
            term = nn(d_ref[(x + s + 3 * y) % 4, rows, :], held[i])
            if i == 0:
                out_ref[...] = term
            else:
                out_ref[...] += term


def weights(own_half, l_blocks, d_blocks, ready):
    vmem = pl.BlockSpec(memory_space=pltpu.VMEM)
    return call(
        functools.partial(weights_kernel, own_half),
        struct((2 * HD, WIDTH // 2), f32),
        (*l_blocks, d_blocks, ready),
        megabytes=57,
        micros=2,
        in_specs=[pl.BlockSpec(memory_space=pl.ANY)] * 8 + [vmem] * 2,
        scratch_shapes=[pltpu.VMEM((8, ROWS, WIDTH // 2), bf16), pltpu.SemaphoreType.DMA((8,))],
    )


def finish_kernel(mine_ref, got_ref, k_ref, v_ref):
    total = mine_ref[...] + got_ref[...]
    k_ref[...] = total[:HD, :].T
    v_ref[...] = total[HD:, :].T


def on_device(queries, key_states, value_states, attn_output, output_grad, log_norms, layer_input, doc_lengths):
    q_par, do_par = (send(a, other_core) for a in (queries, output_grad))
    l_own = send(layer_input, spread)
    kv, aux_own = prepare(doc_lengths, key_states, value_states, output_grad, attn_output, log_norms)
    kv, aux_own, q_par, do_par = together(kv, aux_own, q_par, do_par)
    aux_par = send(aux_own, other_core)
    kv, aux_par = together(kv, aux_par)
    aux, q, do = (aux_own, aux_par), (queries, q_par), (output_grad, do_par)

    kv_far, kv_y, kv_zl = (send(kv, within_half(flip, True)) for flip in (3, 2, 1))

    behind, ahead, across = shifted(dx=-1), shifted(dx=1), shifted(dz=2)
    *dqs, dkv_own = attention((0,), (kv,), aux, q, do, None, (f32, f32), f32, 0.3)
    l_own, dkv_own, kv_y, kv_far, kv_zl, *dqs = together(l_own, dkv_own, kv_y, kv_far, kv_zl, *dqs)
    own_1, own_3, other_0 = (send(l_own, t) for t in (behind, ahead, across))

    *dqs, dkv_far = attention((4, 6), (kv_y, kv_far), aux, q, do, dqs, (f32, f32), bf16, 0.3)
    got_far = send(dkv_far, within_half(2, False))
    dq_own, dq_par, dkv_zl = attention((2,), (kv_zl,), aux, q, do, dqs, (f32, bf16), f32, 1.5)
    dq_own, dq_par, dkv_zl, got_far, l_own, own_1, own_3, other_0 = together(
        dq_own, dq_par, dkv_zl, got_far, l_own, own_1, own_3, other_0
    )
    pair = (2 * ROWS, 2 * HD)
    dkv, dkv_low = call(add_kernel, (struct(pair, f32), struct(pair, bf16)), (dkv_own, dkv_zl, got_far))
    got_zl = send(dkv_low, other_zl)
    other_0, own_1, _ = together(other_0, own_1, dkv_low)
    other_3, own_2, other_1 = send(other_0, ahead), send(own_1, behind), send(other_0, behind)
    d_copies = call(close_kernel, struct((4, 4 * HD, ROWS), bf16), (dkv, got_zl))
    columns = [[y * 4 + rest for y in range(4)] for rest in range(4)]
    d_blocks = lax.all_to_all(d_copies, "ctx", 0, 0, axis_index_groups=columns)

    other_3, dq_par, _ = together(other_3, dq_par, d_copies)
    other_2 = send(other_3, ahead)
    dq_got = send(dq_par, other_core)
    query_grad = ((dq_own + dq_got.astype(f32)) * SCALE).astype(bf16)
    ready = arrived((own_2, other_1), 4)
    l_blocks = (l_own, other_0, own_1, other_1, own_2, other_2, own_3, other_3)
    sent = weights(False, l_blocks, d_blocks, ready)
    got = send(sent, other_core)
    kept = weights(True, l_blocks, d_blocks, ready)
    key_weight, value_weight = call(
        finish_kernel, (struct((WIDTH // 2, HD), f32),) * 2, (kept, got)
    )
    return query_grad, key_weight, value_weight


def solution(mesh):
    placed = (
        P("ctx", "tp"),
        P("ctx", "tp"),
        P("ctx", "tp"),
        P("ctx", "tp"),
        P("ctx", "tp"),
        P("tp", "ctx"),
        P("ctx", "tp"),
        P(),
    )
    return jax.shard_map(
        on_device,
        mesh=mesh,
        in_specs=placed,
        out_specs=(P("ctx", "tp"), P("ctx", "tp"), P("ctx", "tp")),
        check_vma=False,
    )
```

```python
import functools
import itertools
import math

import jax
import jax.numpy as jnp
from jax import lax
from jax.experimental import pallas as pl
from jax.experimental.pallas import tpu as pltpu
from jax.sharding import PartitionSpec as P

HD = 128
HEADS = 8
ROWS = 256
WIDTH = HEADS * HD
SCALE = 1.0 / math.sqrt(HD)
LOG2E = math.log2(math.e)
AXES = ("ctx", "tp")
DOCS = 16
STEP_HEADS = 4

f32 = jnp.float32
bf16 = jnp.bfloat16


def linear(x, y, z, core):
    zh, zl = divmod(z, 2)
    return ((y * 2 + zl) * 2 + core) * 8 + x * 2 + zh


def route(target):
    pairs = []
    for x, y, z, core in itertools.product(range(4), range(4), range(4), range(2)):
        to = target(x, y, z, core)
        if to is not None:
            pairs.append((linear(x, y, z, core), linear(*to)))
    return pairs


def send(value, target):
    return lax.ppermute(value, AXES, route(target))


def other_core(x, y, z, core):
    return (x, y, z, 1 - core)


def shifted(dx=0, dy=0, dz=0):
    return lambda x, y, z, core: ((x + dx) % 4, (y + dy) % 4, (z + dz) % 4, core)


def other_zl(x, y, z, core):
    return (x, y, z ^ 1, core)


def spread(x, y, z, core):
    zh, zl = divmod(z, 2)
    return ((x + y) % 4, x, zl * 2 + zh, core)


def within_half(flip, later):
    def target(x, y, z, core):
        place = (y % 2) * 2 + z % 2
        to = place ^ flip
        if (to > place) != later:
            return None
        return (x, y - y % 2 + to // 2, z - z % 2 + to % 2, core)

    return target


def nt(a, b):
    return lax.dot_general(a, b, (((1,), (1,)), ((), ())), preferred_element_type=f32)


def nn(a, b):
    return lax.dot_general(a, b, (((1,), (0,)), ((), ())), preferred_element_type=f32)


def tn(a, b):
    return lax.dot_general(a, b, (((0,), (0,)), ((), ())), preferred_element_type=f32)


def together(*arrays):
    return lax.optimization_barrier(arrays)


def call(kernel, out_shape, operands, megabytes=12, micros=0.01, **more):
    return pl.pallas_call(
        kernel,
        out_shape=out_shape,
        compiler_params=pltpu.CompilerParams(vmem_limit_bytes=megabytes << 20),
        cost_estimate=pl.CostEstimate(flops=int(micros * 1.15e9), bytes_accessed=1 << 16, transcendentals=0),
        **more,
    )(*operands)


def struct(shape, dtype):
    return jax.ShapeDtypeStruct(shape, dtype)


def arrived_kernel(*refs):
    refs[-1][...] = jnp.zeros_like(refs[-1])


def arrived(arrays, micros):
    return call(
        arrived_kernel,
        struct((8, 128), f32),
        arrays,
        micros=micros,
        in_specs=[pl.BlockSpec(memory_space=pl.ANY)] * len(arrays),
    )


def prepare_kernel(lengths_ref, k_any, v_any, do_any, out_any, ln_any, kv_ref, aux_ref, do_ref, out_ref, sems):
    copies = [
        pltpu.make_async_copy(src, dst, sems.at[i])
        for i, (src, dst) in enumerate(
            (
                (k_any, kv_ref.at[:, :HD]),
                (v_any, kv_ref.at[:, HD:]),
                (ln_any, aux_ref.at[HEADS : 2 * HEADS, :]),
                (do_any, do_ref),
                (out_any, out_ref),
            )
        )
    ]
    for copy in copies:
        copy.start()
    positions = lax.axis_index("ctx") * ROWS + lax.broadcasted_iota(jnp.int32, (HEADS, ROWS), 1)
    end = jnp.int32(0)
    first = jnp.zeros((HEADS, ROWS), jnp.int32)
    for i in range(DOCS):
        end = end + lengths_ref[i]
        first = jnp.where(positions >= end, end, first)
    aux_ref[2 * HEADS :, :] = first.astype(f32)
    for copy in copies:
        copy.wait()
    aux_ref[HEADS : 2 * HEADS, :] = aux_ref[HEADS : 2 * HEADS, :] * LOG2E
    for h in range(HEADS):
        cols = slice(h * HD, (h + 1) * HD)
        prod = do_ref[:, cols].astype(f32) * out_ref[:, cols].astype(f32)
        aux_ref[h : h + 1, :] = jnp.sum(prod.T, axis=0, keepdims=True)


def prepare(doc_lengths, k, v, do, out, ln):
    return call(
        prepare_kernel,
        (struct((ROWS, 2 * HD), bf16), struct((3 * HEADS, ROWS), f32)),
        (doc_lengths, k, v, do, out, ln),
        in_specs=[pl.BlockSpec(memory_space=pltpu.SMEM)] + [pl.BlockSpec(memory_space=pltpu.HBM)] * 5,
        megabytes=56,
        micros=0.3,
        scratch_shapes=[pltpu.VMEM((ROWS, WIDTH), bf16)] * 2 + [pltpu.SemaphoreType.DMA((5,))],
    )


def attention_kernel(flips, has_sum, *refs):
    refs = list(refs)
    take = lambda n: [refs.pop(0) for _ in range(n)]
    kv_refs, aux_refs, q_refs, do_refs = take(len(flips)), take(2), take(2), take(2)
    sums = take(2) if has_sum else None
    dq_refs = take(2)
    dkv_ref, dk_acc, dv_acc = refs
    me = lax.axis_index("ctx")
    dk_acc[...] = jnp.zeros_like(dk_acc)
    dv_acc[...] = jnp.zeros_like(dv_acc)

    @pl.loop(0, HEADS // STEP_HEADS)
    def _(step):
        k = jnp.concatenate([r[:, :HD] for r in kv_refs], axis=0)
        v = jnp.concatenate([r[:, HD:] for r in kv_refs], axis=0)
        offset = lax.broadcasted_iota(jnp.int32, (ROWS, 1), 0)
        key_pos = jnp.concatenate([(me ^ flip) * ROWS + offset for flip in flips], axis=0)
        lane = lax.broadcasted_iota(jnp.int32, (1, ROWS), 1)
        dk = dv = None
        for i in range(2):
            query_pos = (me ^ i) * ROWS + lane
            first = aux_refs[i][2 * HEADS : 2 * HEADS + 1, :].astype(jnp.int32)
            visible = (key_pos <= query_pos) & (key_pos >= first)
            for j in range(STEP_HEADS):
                h = step * STEP_HEADS + j
                cols = pl.ds(pl.multiple_of(h * HD, HD), HD)
                q = q_refs[i][:, cols]
                do = do_refs[i][:, cols]
                dots = aux_refs[i][pl.ds(h, 1), :]
                norm = aux_refs[i][pl.ds(HEADS + h, 1), :]
                p = jnp.where(visible, jnp.exp2(nt(k, q) * (SCALE * LOG2E) - norm), 0.0)
                ds = (p * (nt(v, do) - dots)).astype(bf16)
                dv_term, dk_term, dq = nn(p.astype(bf16), do), nn(ds, q), tn(ds, k)
                dv = dv_term if dv is None else dv + dv_term
                dk = dk_term if dk is None else dk + dk_term
                if has_sum:
                    dq = dq + sums[i][:, cols]
                dq_refs[i][:, cols] = dq.astype(dq_refs[i].dtype)
        dk_acc[...] += dk
        dv_acc[...] += dv

    dkv_ref[:, :HD] = dk_acc[...].astype(dkv_ref.dtype)
    dkv_ref[:, HD:] = dv_acc[...].astype(dkv_ref.dtype)


def attention(flips, kv, aux, q, do, sums, dq_types, dkv_type, micros):
    keys = len(flips) * ROWS
    return call(
        functools.partial(attention_kernel, flips, sums is not None),
        (
            struct((ROWS, WIDTH), dq_types[0]),
            struct((ROWS, WIDTH), dq_types[1]),
            struct((keys, 2 * HD), dkv_type),
        ),
        [*kv, *aux, *q, *do, *(sums or ())],
        megabytes=14,
        micros=micros,
        scratch_shapes=[pltpu.VMEM((keys, HD), f32)] * 2,
    )


def add_kernel(own_ref, zl_ref, got_ref, sum_ref, low_ref):
    for half, near_ref in enumerate((own_ref, zl_ref)):
        rows = slice(half * ROWS, (half + 1) * ROWS)
        total = near_ref[...] + got_ref[rows, :].astype(f32)
        sum_ref[rows, :] = total
        low_ref[rows, :] = total.astype(bf16)


def close_kernel(sum_ref, got_ref, d_ref):
    for half in range(2):
        mine = slice(half * ROWS, (half + 1) * ROWS)
        its = slice((1 - half) * ROWS, (2 - half) * ROWS)
        total = sum_ref[mine, :] + got_ref[its, :].astype(f32)
        k_grad = (total[:, :HD] * SCALE).T.astype(bf16)
        v_grad = total[:, HD:].T.astype(bf16)
        d_ref[half * 2 * HD : half * 2 * HD + HD, :] = k_grad
        d_ref[half * 2 * HD + HD : (half + 1) * 2 * HD, :] = v_grad


def weights_kernel(*refs):
    l_refs, d_refs, (_, sent_ref, kept_ref, d_all) = refs[:8], refs[8:12], refs[12:]
    me, tp = lax.axis_index("ctx"), lax.axis_index("tp")
    core, zl, y = me % 2, (me // 2) % 2, me // 4
    x, zh = tp // 2, tp % 2
    for r in range(4):
        d_all[r] = d_refs[r][...]
    half_width = WIDTH // 2
    for out_ref, whose in ((sent_ref, 1 - core), (kept_ref, core)):
        for t in range(2):
            tile = half_width // 2
            cols = pl.ds(pl.multiple_of(whose * half_width + t * tile, tile), tile)
            total = None
            for s in range(4):
                for j in range(2):
                    rows = pl.ds(pl.multiple_of(((zh ^ j) ^ zl) * 2 * HD, 2 * HD), 2 * HD)
                    term = nn(d_all[(x + s + 2 * y) % 4, rows, :], l_refs[s * 2 + j][:, cols])
                    total = term if total is None else total + term
            out_ref[:, t * tile : (t + 1) * tile] = total


def weights(l_blocks, d_blocks, ready):
    return call(
        weights_kernel,
        (struct((2 * HD, WIDTH // 2), f32),) * 2,
        (*l_blocks, *d_blocks, ready),
        scratch_shapes=[pltpu.VMEM((4, 4 * HD, ROWS), bf16)],
    )


def finish_kernel(mine_ref, got_ref, k_ref, v_ref):
    total = mine_ref[...] + got_ref[...]
    k_ref[...] = total[:HD, :].T
    v_ref[...] = total[HD:, :].T


def on_device(queries, key_states, value_states, attn_output, output_grad, log_norms, layer_input, doc_lengths):
    q_par, do_par = (send(a, other_core) for a in (queries, output_grad))
    l_own = send(layer_input, spread)
    kv, aux_own = prepare(doc_lengths, key_states, value_states, output_grad, attn_output, log_norms)
    kv, aux_own, q_par, do_par = together(kv, aux_own, q_par, do_par)
    aux_par = send(aux_own, other_core)
    kv, aux_par = together(kv, aux_par)
    aux, q, do = (aux_own, aux_par), (queries, q_par), (output_grad, do_par)

    kv_far, kv_y, kv_zl = (send(kv, within_half(flip, True)) for flip in (3, 2, 1))

    behind, ahead, across = shifted(dx=-1), shifted(dx=1), shifted(dz=2)
    *dqs, dkv_own = attention((0,), (kv,), aux, q, do, None, (f32, f32), f32, 0.3)
    l_own, dkv_own, kv_y, kv_far, kv_zl, *dqs = together(l_own, dkv_own, kv_y, kv_far, kv_zl, *dqs)
    own_1, own_3, other_0 = (send(l_own, t) for t in (behind, ahead, across))

    *dqs, dkv_far = attention((4, 6), (kv_y, kv_far), aux, q, do, dqs, (f32, f32), bf16, 0.3)
    got_far = send(dkv_far, within_half(2, False))
    dq_own, dq_par, dkv_zl = attention((2,), (kv_zl,), aux, q, do, dqs, (f32, bf16), f32, 1.5)
    dq_own, dq_par, dkv_zl, got_far, l_own, own_1, own_3, other_0 = together(
        dq_own, dq_par, dkv_zl, got_far, l_own, own_1, own_3, other_0
    )
    pair = (2 * ROWS, 2 * HD)
    dkv, dkv_low = call(add_kernel, (struct(pair, f32), struct(pair, bf16)), (dkv_own, dkv_zl, got_far))
    got_zl = send(dkv_low, other_zl)
    other_0, dq_par, _ = together(other_0, dq_par, dkv_low)
    other_3, other_1 = send(other_0, ahead), send(other_0, behind)
    dq_got = send(dq_par, other_core)
    query_grad = ((dq_own + dq_got.astype(f32)) * SCALE).astype(bf16)
    got_zl, query_grad = together(got_zl, query_grad)
    d_own = call(close_kernel, struct((4 * HD, ROWS), bf16), (dkv, got_zl))
    d_2, d_1, d_3 = (send(d_own, shifted(dy=-dy)) for dy in (2, 1, 3))
    ready = arrived((d_1, d_2, d_3), 8)

    other_3, other_1, own_1, _ = together(other_3, other_1, own_1, d_own)
    own_2, other_2 = send(own_1, behind), send(other_3, ahead)
    l_blocks = (l_own, other_0, own_1, other_1, own_2, other_2, own_3, other_3)
    d_blocks = (d_own, d_1, d_2, d_3)
    sent, kept = weights(l_blocks, d_blocks, ready)
    got = send(sent, other_core)
    key_weight, value_weight = call(
        finish_kernel, (struct((WIDTH // 2, HD), f32),) * 2, (kept, got)
    )
    return query_grad, key_weight, value_weight


def solution(mesh):
    placed = (
        P("ctx", "tp"),
        P("ctx", "tp"),
        P("ctx", "tp"),
        P("ctx", "tp"),
        P("ctx", "tp"),
        P("tp", "ctx"),
        P("ctx", "tp"),
        P(),
    )
    return jax.shard_map(
        on_device,
        mesh=mesh,
        in_specs=placed,
        out_specs=(P("ctx", "tp"), P("ctx", "tp"), P("ctx", "tp")),
        check_vma=False,
    )
```

```python
import functools
import itertools
import math

import jax
import jax.numpy as jnp
from jax import lax
from jax.experimental import pallas as pl
from jax.experimental.pallas import tpu as pltpu
from jax.sharding import PartitionSpec as P

HD = 128
HEADS = 8
ROWS = 256
WIDTH = HEADS * HD
SCALE = 1.0 / math.sqrt(HD)
LOG2E = math.log2(math.e)
AXES = ("ctx", "tp")
DOCS = 16
STEP_HEADS = 8
GROUP = 16

f32 = jnp.float32
bf16 = jnp.bfloat16


def linear(x, y, z, core):
    zh, zl = divmod(z, 2)
    return ((y * 2 + zl) * 2 + core) * 8 + x * 2 + zh


def route(target):
    pairs = []
    for x, y, z, core in itertools.product(range(4), range(4), range(4), range(2)):
        to = target(x, y, z, core)
        if to is not None:
            pairs.append((linear(x, y, z, core), linear(*to)))
    return pairs


def send(value, target):
    return lax.ppermute(value, AXES, route(target))


def other_core(x, y, z, core):
    return (x, y, z, 1 - core)


def shifted(dx=0, dy=0, dz=0):
    return lambda x, y, z, core: ((x + dx) % 4, (y + dy) % 4, (z + dz) % 4, core)


def other_zl(x, y, z, core):
    return (x, y, z ^ 1, core)


def spread(x, y, z, core):
    zh, zl = divmod(z, 2)
    return ((x + y) % 4, x, zl * 2 + zh, core)


def within_half(flip, later):
    def target(x, y, z, core):
        place = (y % 2) * 2 + z % 2
        to = place ^ flip
        if (to > place) != later:
            return None
        return (x, y - y % 2 + to // 2, z - z % 2 + to % 2, core)

    return target


def nt(a, b):
    return lax.dot_general(a, b, (((1,), (1,)), ((), ())), preferred_element_type=f32)


def nn(a, b):
    return lax.dot_general(a, b, (((1,), (0,)), ((), ())), preferred_element_type=f32)


def tn(a, b):
    return lax.dot_general(a, b, (((0,), (0,)), ((), ())), preferred_element_type=f32)


def together(*arrays):
    return lax.optimization_barrier(arrays)


def call(kernel, out_shape, operands, megabytes=12, micros=0.01, **more):
    return pl.pallas_call(
        kernel,
        out_shape=out_shape,
        compiler_params=pltpu.CompilerParams(vmem_limit_bytes=megabytes << 20),
        cost_estimate=pl.CostEstimate(flops=int(micros * 1.15e9), bytes_accessed=1 << 16, transcendentals=0),
        **more,
    )(*operands)


def struct(shape, dtype):
    return jax.ShapeDtypeStruct(shape, dtype)


def arrived_kernel(*refs):
    refs[-1][...] = jnp.zeros_like(refs[-1])


def arrived(arrays, micros):
    return call(
        arrived_kernel,
        struct((8, 128), f32),
        arrays,
        micros=micros,
        in_specs=[pl.BlockSpec(memory_space=pl.ANY)] * len(arrays),
    )


def prepare_kernel(lengths_ref, k_any, v_any, do_any, out_any, ln_any, kv_ref, aux_ref, do_ref, out_ref, sems):
    copies = [
        pltpu.make_async_copy(src, dst, sems.at[i])
        for i, (src, dst) in enumerate(
            (
                (k_any, kv_ref.at[:, :HD]),
                (v_any, kv_ref.at[:, HD:]),
                (ln_any, aux_ref.at[HEADS : 2 * HEADS, :]),
                (do_any, do_ref),
                (out_any, out_ref),
            )
        )
    ]
    for copy in copies:
        copy.start()
    positions = lax.axis_index("ctx") * ROWS + lax.broadcasted_iota(jnp.int32, (HEADS, ROWS), 1)
    end = jnp.int32(0)
    first = jnp.zeros((HEADS, ROWS), jnp.int32)
    for i in range(DOCS):
        end = end + lengths_ref[i]
        first = jnp.where(positions >= end, end, first)
    aux_ref[2 * HEADS :, :] = first.astype(f32)
    for copy in copies:
        copy.wait()
    aux_ref[HEADS : 2 * HEADS, :] = aux_ref[HEADS : 2 * HEADS, :] * LOG2E
    for h in range(HEADS):
        cols = slice(h * HD, (h + 1) * HD)
        prod = do_ref[:, cols].astype(f32) * out_ref[:, cols].astype(f32)
        aux_ref[h : h + 1, :] = jnp.sum(prod.T, axis=0, keepdims=True)


def prepare(doc_lengths, k, v, do, out, ln):
    return call(
        prepare_kernel,
        (struct((ROWS, 2 * HD), bf16), struct((3 * HEADS, ROWS), f32)),
        (doc_lengths, k, v, do, out, ln),
        in_specs=[pl.BlockSpec(memory_space=pltpu.SMEM)] + [pl.BlockSpec(memory_space=pltpu.HBM)] * 5,
        megabytes=56,
        micros=0.3,
        scratch_shapes=[pltpu.VMEM((ROWS, WIDTH), bf16)] * 2 + [pltpu.SemaphoreType.DMA((5,))],
    )


def attention_kernel(flips, has_sum, *refs):
    refs = list(refs)
    take = lambda n: [refs.pop(0) for _ in range(n)]
    kv_refs, aux_refs, q_refs, do_refs = take(len(flips)), take(2), take(2), take(2)
    sums = take(2) if has_sum else None
    dq_refs = take(2)
    dkv_ref, dk_acc, dv_acc = refs
    me = lax.axis_index("ctx")
    dk_acc[...] = jnp.zeros_like(dk_acc)
    dv_acc[...] = jnp.zeros_like(dv_acc)

    @pl.loop(0, HEADS // STEP_HEADS)
    def _(step):
        k = jnp.concatenate([r[:, :HD] for r in kv_refs], axis=0)
        v = jnp.concatenate([r[:, HD:] for r in kv_refs], axis=0)
        offset = lax.broadcasted_iota(jnp.int32, (ROWS, 1), 0)
        key_pos = jnp.concatenate([(me ^ flip) * ROWS + offset for flip in flips], axis=0)
        lane = lax.broadcasted_iota(jnp.int32, (1, ROWS), 1)
        tiles = []
        for i in range(2):
            query_pos = (me ^ i) * ROWS + lane
            first = aux_refs[i][2 * HEADS : 2 * HEADS + 1, :].astype(jnp.int32)
            visible = (key_pos <= query_pos) & (key_pos >= first)
            for j in range(STEP_HEADS):
                h = step * STEP_HEADS + j
                cols = pl.ds(pl.multiple_of(h * HD, HD), HD)
                dots = aux_refs[i][pl.ds(h, 1), :]
                norm = aux_refs[i][pl.ds(HEADS + h, 1), :]
                tiles.append((i, cols, visible, dots, norm))
        dk = dv = None
        for start in range(0, len(tiles), GROUP):
            group = tiles[start : start + GROUP]
            products = []
            for i, cols, *_ in group:
                q, do = q_refs[i][:, cols], do_refs[i][:, cols]
                products.append((q, do, nt(k, q), nt(v, do)))
            low = []
            for (_, _, visible, dots, norm), (_, _, score, prob_grad) in zip(group, products):
                p = jnp.where(visible, jnp.exp2(score * (SCALE * LOG2E) - norm), 0.0)
                low.append((p.astype(bf16), (p * (prob_grad - dots)).astype(bf16)))
            for (i, cols, *_), (q, do, *_), (p, ds) in zip(group, products, low):
                dv_term, dk_term, dq = nn(p, do), nn(ds, q), tn(ds, k)
                dv = dv_term if dv is None else dv + dv_term
                dk = dk_term if dk is None else dk + dk_term
                if has_sum:
                    dq = dq + sums[i][:, cols]
                dq_refs[i][:, cols] = dq.astype(dq_refs[i].dtype)
        dk_acc[...] += dk
        dv_acc[...] += dv

    dkv_ref[:, :HD] = dk_acc[...].astype(dkv_ref.dtype)
    dkv_ref[:, HD:] = dv_acc[...].astype(dkv_ref.dtype)


def attention(flips, kv, aux, q, do, sums, dq_types, dkv_type, micros):
    keys = len(flips) * ROWS
    return call(
        functools.partial(attention_kernel, flips, sums is not None),
        (
            struct((ROWS, WIDTH), dq_types[0]),
            struct((ROWS, WIDTH), dq_types[1]),
            struct((keys, 2 * HD), dkv_type),
        ),
        [*kv, *aux, *q, *do, *(sums or ())],
        megabytes=24,
        micros=micros,
        scratch_shapes=[pltpu.VMEM((keys, HD), f32)] * 2,
    )


def add_kernel(own_ref, zl_ref, got_ref, sum_ref, low_ref):
    for half, near_ref in enumerate((own_ref, zl_ref)):
        rows = slice(half * ROWS, (half + 1) * ROWS)
        total = near_ref[...] + got_ref[rows, :].astype(f32)
        sum_ref[rows, :] = total
        low_ref[rows, :] = total.astype(bf16)


def close_kernel(sum_ref, got_ref, d_ref):
    for half in range(2):
        mine = slice(half * ROWS, (half + 1) * ROWS)
        its = slice((1 - half) * ROWS, (2 - half) * ROWS)
        total = sum_ref[mine, :] + got_ref[its, :].astype(f32)
        k_grad = (total[:, :HD] * SCALE).T.astype(bf16)
        v_grad = total[:, HD:].T.astype(bf16)
        d_ref[half * 2 * HD : half * 2 * HD + HD, :] = k_grad
        d_ref[half * 2 * HD + HD : (half + 1) * 2 * HD, :] = v_grad


def weights_kernel(*refs):
    l_refs, d_refs, (_, sent_ref, kept_ref, d_all) = refs[:8], refs[8:12], refs[12:]
    me, tp = lax.axis_index("ctx"), lax.axis_index("tp")
    core, zl, y = me % 2, (me // 2) % 2, me // 4
    x, zh = tp // 2, tp % 2
    for r in range(4):
        d_all[r] = d_refs[r][...]
    half_width = WIDTH // 2
    for out_ref, whose in ((sent_ref, 1 - core), (kept_ref, core)):
        for t in range(2):
            tile = half_width // 2
            cols = pl.ds(pl.multiple_of(whose * half_width + t * tile, tile), tile)
            total = None
            for s in range(4):
                for j in range(2):
                    rows = pl.ds(pl.multiple_of(((zh ^ j) ^ zl) * 2 * HD, 2 * HD), 2 * HD)
                    term = nn(d_all[(x + s + 2 * y) % 4, rows, :], l_refs[s * 2 + j][:, cols])
                    total = term if total is None else total + term
            out_ref[:, t * tile : (t + 1) * tile] = total


def weights(l_blocks, d_blocks, ready):
    return call(
        weights_kernel,
        (struct((2 * HD, WIDTH // 2), f32),) * 2,
        (*l_blocks, *d_blocks, ready),
        scratch_shapes=[pltpu.VMEM((4, 4 * HD, ROWS), bf16)],
    )


def finish_kernel(mine_ref, got_ref, k_ref, v_ref):
    total = mine_ref[...] + got_ref[...]
    k_ref[...] = total[:HD, :].T
    v_ref[...] = total[HD:, :].T


def on_device(queries, key_states, value_states, attn_output, output_grad, log_norms, layer_input, doc_lengths):
    q_par, do_par = (send(a, other_core) for a in (queries, output_grad))
    l_own = send(layer_input, spread)
    kv, aux_own = prepare(doc_lengths, key_states, value_states, output_grad, attn_output, log_norms)
    kv, aux_own, q_par, do_par = together(kv, aux_own, q_par, do_par)
    aux_par = send(aux_own, other_core)
    kv, aux_par = together(kv, aux_par)
    aux, q, do = (aux_own, aux_par), (queries, q_par), (output_grad, do_par)

    kv_far, kv_y, kv_zl = (send(kv, within_half(flip, True)) for flip in (3, 2, 1))

    behind, ahead, across = shifted(dx=-1), shifted(dx=1), shifted(dz=2)
    *dqs, dkv_own = attention((0,), (kv,), aux, q, do, None, (f32, f32), f32, 0.3)
    l_own, dkv_own, kv_y, kv_far, kv_zl, *dqs = together(l_own, dkv_own, kv_y, kv_far, kv_zl, *dqs)
    own_1, own_3, other_0 = (send(l_own, t) for t in (behind, ahead, across))

    *dqs, dkv_far = attention((4, 6), (kv_y, kv_far), aux, q, do, dqs, (f32, f32), bf16, 0.3)
    got_far = send(dkv_far, within_half(2, False))
    dq_own, dq_par, dkv_zl = attention((2,), (kv_zl,), aux, q, do, dqs, (f32, bf16), f32, 1.5)
    dq_own, dq_par, dkv_zl, got_far, l_own, own_1, own_3, other_0 = together(
        dq_own, dq_par, dkv_zl, got_far, l_own, own_1, own_3, other_0
    )
    pair = (2 * ROWS, 2 * HD)
    dkv, dkv_low = call(add_kernel, (struct(pair, f32), struct(pair, bf16)), (dkv_own, dkv_zl, got_far))
    got_zl = send(dkv_low, other_zl)
    other_0, dq_par, _ = together(other_0, dq_par, dkv_low)
    other_3, other_1 = send(other_0, ahead), send(other_0, behind)
    dq_got = send(dq_par, other_core)
    query_grad = ((dq_own + dq_got.astype(f32)) * SCALE).astype(bf16)
    got_zl, query_grad = together(got_zl, query_grad)
    d_own = call(close_kernel, struct((4 * HD, ROWS), bf16), (dkv, got_zl))
    d_2, d_1, d_3 = (send(d_own, shifted(dy=-dy)) for dy in (2, 1, 3))
    ready = arrived((d_1, d_2, d_3), 8)

    other_3, other_1, own_1, _ = together(other_3, other_1, own_1, d_own)
    own_2, other_2 = send(own_1, behind), send(other_3, ahead)
    l_blocks = (l_own, other_0, own_1, other_1, own_2, other_2, own_3, other_3)
    d_blocks = (d_own, d_1, d_2, d_3)
    sent, kept = weights(l_blocks, d_blocks, ready)
    got = send(sent, other_core)
    key_weight, value_weight = call(
        finish_kernel, (struct((WIDTH // 2, HD), f32),) * 2, (kept, got)
    )
    return query_grad, key_weight, value_weight


def solution(mesh):
    placed = (
        P("ctx", "tp"),
        P("ctx", "tp"),
        P("ctx", "tp"),
        P("ctx", "tp"),
        P("ctx", "tp"),
        P("tp", "ctx"),
        P("ctx", "tp"),
        P(),
    )
    return jax.shard_map(
        on_device,
        mesh=mesh,
        in_specs=placed,
        out_specs=(P("ctx", "tp"), P("ctx", "tp"), P("ctx", "tp")),
        check_vma=False,
    )
```

```python
import functools
import itertools
import math

import jax
import jax.numpy as jnp
from jax import lax
from jax.experimental import pallas as pl
from jax.experimental.pallas import tpu as pltpu
from jax.sharding import PartitionSpec as P

HD = 128
HEADS = 8
ROWS = 256
WIDTH = HEADS * HD
SCALE = 1.0 / math.sqrt(HD)
LOG2E = math.log2(math.e)
AXES = ("ctx", "tp")
DOCS = 16
STEP_HEADS = 8
GROUP = 16

f32 = jnp.float32
bf16 = jnp.bfloat16


def linear(x, y, z, core):
    zh, zl = divmod(z, 2)
    return ((y * 2 + zl) * 2 + core) * 8 + x * 2 + zh


def route(target):
    pairs = []
    for x, y, z, core in itertools.product(range(4), range(4), range(4), range(2)):
        to = target(x, y, z, core)
        if to is not None:
            pairs.append((linear(x, y, z, core), linear(*to)))
    return pairs


def send(value, target):
    return lax.ppermute(value, AXES, route(target))


def other_core(x, y, z, core):
    return (x, y, z, 1 - core)


def shifted(dx=0, dy=0, dz=0):
    return lambda x, y, z, core: ((x + dx) % 4, (y + dy) % 4, (z + dz) % 4, core)


def other_zl(x, y, z, core):
    return (x, y, z ^ 1, core)


def spread(x, y, z, core):
    zh, zl = divmod(z, 2)
    return ((x + y) % 4, x, zl * 2 + zh, core)


def within_half(flip, later):
    def target(x, y, z, core):
        place = (y % 2) * 2 + z % 2
        to = place ^ flip
        if (to > place) != later:
            return None
        return (x, y - y % 2 + to // 2, z - z % 2 + to % 2, core)

    return target


def nt(a, b):
    return lax.dot_general(a, b, (((1,), (1,)), ((), ())), preferred_element_type=f32)


def nn(a, b):
    return lax.dot_general(a, b, (((1,), (0,)), ((), ())), preferred_element_type=f32)


def tn(a, b):
    return lax.dot_general(a, b, (((0,), (0,)), ((), ())), preferred_element_type=f32)


def together(*arrays):
    return lax.optimization_barrier(arrays)


def call(kernel, out_shape, operands, megabytes=12, micros=0.01, **more):
    return pl.pallas_call(
        kernel,
        out_shape=out_shape,
        compiler_params=pltpu.CompilerParams(vmem_limit_bytes=megabytes << 20),
        cost_estimate=pl.CostEstimate(flops=int(micros * 1.15e9), bytes_accessed=1 << 16, transcendentals=0),
        **more,
    )(*operands)


def struct(shape, dtype):
    return jax.ShapeDtypeStruct(shape, dtype)


def arrived_kernel(*refs):
    refs[-1][...] = jnp.zeros_like(refs[-1])


def arrived(arrays, micros):
    return call(
        arrived_kernel,
        struct((8, 128), f32),
        arrays,
        micros=micros,
        in_specs=[pl.BlockSpec(memory_space=pl.ANY)] * len(arrays),
    )


def prepare_kernel(lengths_ref, k_any, v_any, do_any, out_any, ln_any, kv_ref, aux_ref, do_ref, out_ref, sems):
    copies = [
        pltpu.make_async_copy(src, dst, sems.at[i])
        for i, (src, dst) in enumerate(
            (
                (k_any, kv_ref.at[:, :HD]),
                (v_any, kv_ref.at[:, HD:]),
                (ln_any, aux_ref.at[HEADS : 2 * HEADS, :]),
                (do_any, do_ref),
                (out_any, out_ref),
            )
        )
    ]
    for copy in copies:
        copy.start()
    positions = lax.axis_index("ctx") * ROWS + lax.broadcasted_iota(jnp.int32, (HEADS, ROWS), 1)
    end = jnp.int32(0)
    first = jnp.zeros((HEADS, ROWS), jnp.int32)
    for i in range(DOCS):
        end = end + lengths_ref[i]
        first = jnp.where(positions >= end, end, first)
    aux_ref[2 * HEADS :, :] = first.astype(f32)
    for copy in copies:
        copy.wait()
    aux_ref[HEADS : 2 * HEADS, :] = aux_ref[HEADS : 2 * HEADS, :] * LOG2E
    for h in range(HEADS):
        cols = slice(h * HD, (h + 1) * HD)
        prod = do_ref[:, cols].astype(f32) * out_ref[:, cols].astype(f32)
        aux_ref[h : h + 1, :] = jnp.sum(prod.T, axis=0, keepdims=True)


def prepare(doc_lengths, k, v, do, out, ln):
    return call(
        prepare_kernel,
        (struct((ROWS, 2 * HD), bf16), struct((3 * HEADS, ROWS), f32)),
        (doc_lengths, k, v, do, out, ln),
        in_specs=[pl.BlockSpec(memory_space=pltpu.SMEM)] + [pl.BlockSpec(memory_space=pltpu.HBM)] * 5,
        megabytes=56,
        micros=0.3,
        scratch_shapes=[pltpu.VMEM((ROWS, WIDTH), bf16)] * 2 + [pltpu.SemaphoreType.DMA((5,))],
    )


def attention_kernel(flips, has_sum, *refs):
    refs = list(refs)
    take = lambda n: [refs.pop(0) for _ in range(n)]
    kv_refs, aux_refs, q_refs, do_refs = take(len(flips)), take(2), take(2), take(2)
    sums = take(2) if has_sum else None
    dq_refs = take(2)
    dkv_ref, dk_acc, dv_acc = refs
    me = lax.axis_index("ctx")
    dk_acc[...] = jnp.zeros_like(dk_acc)
    dv_acc[...] = jnp.zeros_like(dv_acc)

    @pl.loop(0, HEADS // STEP_HEADS)
    def _(step):
        k = jnp.concatenate([r[:, :HD] for r in kv_refs], axis=0)
        v = jnp.concatenate([r[:, HD:] for r in kv_refs], axis=0)
        offset = lax.broadcasted_iota(jnp.int32, (ROWS, 1), 0)
        key_pos = jnp.concatenate([(me ^ flip) * ROWS + offset for flip in flips], axis=0)
        lane = lax.broadcasted_iota(jnp.int32, (1, ROWS), 1)
        tiles = []
        for i in range(2):
            query_pos = (me ^ i) * ROWS + lane
            first = aux_refs[i][2 * HEADS : 2 * HEADS + 1, :].astype(jnp.int32)
            visible = (key_pos <= query_pos) & (key_pos >= first)
            for j in range(STEP_HEADS):
                h = step * STEP_HEADS + j
                cols = pl.ds(pl.multiple_of(h * HD, HD), HD)
                dots = aux_refs[i][pl.ds(h, 1), :]
                norm = aux_refs[i][pl.ds(HEADS + h, 1), :]
                tiles.append((i, cols, visible, dots, norm))
        dk = dv = None
        for start in range(0, len(tiles), GROUP):
            group = tiles[start : start + GROUP]
            products = []
            for i, cols, *_ in group:
                q, do = q_refs[i][:, cols], do_refs[i][:, cols]
                products.append((q, do, nt(k, q), nt(v, do)))
            low = []
            for (_, _, visible, dots, norm), (_, _, score, prob_grad) in zip(group, products):
                p = jnp.where(visible, jnp.exp2(score * (SCALE * LOG2E) - norm), 0.0)
                low.append((p.astype(bf16), (p * (prob_grad - dots)).astype(bf16)))
            for (i, cols, *_), (q, do, *_), (p, ds) in zip(group, products, low):
                dv_term, dk_term, dq = nn(p, do), nn(ds, q), tn(ds, k)
                dv = dv_term if dv is None else dv + dv_term
                dk = dk_term if dk is None else dk + dk_term
                if has_sum:
                    dq = dq + sums[i][:, cols]
                dq_refs[i][:, cols] = dq.astype(dq_refs[i].dtype)
        dk_acc[...] += dk
        dv_acc[...] += dv

    dkv_ref[:, :HD] = dk_acc[...].astype(dkv_ref.dtype)
    dkv_ref[:, HD:] = dv_acc[...].astype(dkv_ref.dtype)


def attention(flips, kv, aux, q, do, sums, dq_types, dkv_type, micros):
    keys = len(flips) * ROWS
    return call(
        functools.partial(attention_kernel, flips, sums is not None),
        (
            struct((ROWS, WIDTH), dq_types[0]),
            struct((ROWS, WIDTH), dq_types[1]),
            struct((keys, 2 * HD), dkv_type),
        ),
        [*kv, *aux, *q, *do, *(sums or ())],
        megabytes=24,
        micros=micros,
        scratch_shapes=[pltpu.VMEM((keys, HD), f32)] * 2,
    )


def add_kernel(own_ref, zl_ref, got_ref, sum_ref, low_ref):
    for half, near_ref in enumerate((own_ref, zl_ref)):
        rows = slice(half * ROWS, (half + 1) * ROWS)
        total = near_ref[...] + got_ref[rows, :].astype(f32)
        sum_ref[rows, :] = total
        low_ref[rows, :] = total.astype(bf16)


def close_kernel(sum_ref, got_ref, d_ref):
    for half in range(2):
        mine = slice(half * ROWS, (half + 1) * ROWS)
        its = slice((1 - half) * ROWS, (2 - half) * ROWS)
        total = sum_ref[mine, :] + got_ref[its, :].astype(f32)
        k_grad = (total[:, :HD] * SCALE).T.astype(bf16)
        v_grad = total[:, HD:].T.astype(bf16)
        d_ref[half * 2 * HD : half * 2 * HD + HD, :] = k_grad
        d_ref[half * 2 * HD + HD : (half + 1) * 2 * HD, :] = v_grad


def weights_kernel(*refs):
    l_refs, d_refs, (_, sent_ref, kept_ref, d_all) = refs[:8], refs[8:12], refs[12:]
    me, tp = lax.axis_index("ctx"), lax.axis_index("tp")
    core, zl, y = me % 2, (me // 2) % 2, me // 4
    x, zh = tp // 2, tp % 2
    for r in range(4):
        d_all[r] = d_refs[r][...]
    half_width = WIDTH // 2
    for out_ref, whose in ((sent_ref, 1 - core), (kept_ref, core)):
        for t in range(2):
            tile = half_width // 2
            cols = pl.ds(pl.multiple_of(whose * half_width + t * tile, tile), tile)
            total = None
            for s in range(4):
                for j in range(2):
                    rows = pl.ds(pl.multiple_of(((zh ^ j) ^ zl) * 2 * HD, 2 * HD), 2 * HD)
                    term = nn(d_all[(x + s + 2 * y) % 4, rows, :], l_refs[s * 2 + j][:, cols])
                    total = term if total is None else total + term
            out_ref[:, t * tile : (t + 1) * tile] = total


def weights(l_blocks, d_blocks, ready):
    return call(
        weights_kernel,
        (struct((2 * HD, WIDTH // 2), f32),) * 2,
        (*l_blocks, *d_blocks, ready),
        scratch_shapes=[pltpu.VMEM((4, 4 * HD, ROWS), bf16)],
    )


def finish_kernel(mine_ref, got_ref, k_ref, v_ref):
    total = mine_ref[...] + got_ref[...]
    k_ref[...] = total[:HD, :].T
    v_ref[...] = total[HD:, :].T


def on_device(queries, key_states, value_states, attn_output, output_grad, log_norms, layer_input, doc_lengths):
    q_par, do_par = (send(a, other_core) for a in (queries, output_grad))
    l_own = send(layer_input, spread)
    kv, aux_own = prepare(doc_lengths, key_states, value_states, output_grad, attn_output, log_norms)
    kv, aux_own, q_par, do_par = together(kv, aux_own, q_par, do_par)
    aux_par = send(aux_own, other_core)
    kv, aux_par = together(kv, aux_par)
    aux, q, do = (aux_own, aux_par), (queries, q_par), (output_grad, do_par)

    kv_far, kv_y, kv_zl = (send(kv, within_half(flip, True)) for flip in (3, 2, 1))

    behind, ahead, across = shifted(dx=-1), shifted(dx=1), shifted(dz=2)
    *dqs, dkv_own = attention((0,), (kv,), aux, q, do, None, (f32, f32), f32, 0.3)
    l_own, dkv_own, kv_y, kv_far, kv_zl, *dqs = together(l_own, dkv_own, kv_y, kv_far, kv_zl, *dqs)
    other_0, own_1, own_3 = (send(l_own, t) for t in (across, behind, ahead))

    *dqs, dkv_far = attention((4, 6), (kv_y, kv_far), aux, q, do, dqs, (f32, f32), bf16, 0.3)
    got_far = send(dkv_far, within_half(2, False))
    dq_own, dq_par, dkv_zl = attention((2,), (kv_zl,), aux, q, do, dqs, (f32, bf16), f32, 1.5)
    other_0, own_1, own_3, l_own, got_far, dkv_zl, dq_own, dq_par = together(
        other_0, own_1, own_3, l_own, got_far, dkv_zl, dq_own, dq_par
    )

    pair = (2 * ROWS, 2 * HD)
    dkv, dkv_low = call(add_kernel, (struct(pair, f32), struct(pair, bf16)), (dkv_own, dkv_zl, got_far))
    got_zl = send(dkv_low, other_zl)
    dq_par, _ = together(dq_par, dkv_low)
    other_3, other_1 = send(other_0, ahead), send(other_0, behind)
    dq_got = send(dq_par, other_core)
    query_grad = ((dq_own + dq_got.astype(f32)) * SCALE).astype(bf16)
    got_zl, query_grad = together(got_zl, query_grad)
    d_own = call(close_kernel, struct((4 * HD, ROWS), bf16), (dkv, got_zl))
    d_2, d_1, d_3 = (send(d_own, shifted(dy=-dy)) for dy in (2, 1, 3))
    ready = arrived((d_1, d_2, d_3), 8)

    other_3, other_1, own_1, _ = together(other_3, other_1, own_1, d_own)
    own_2, other_2 = send(own_1, behind), send(other_3, ahead)
    l_blocks = (l_own, other_0, own_1, other_1, own_2, other_2, own_3, other_3)
    d_blocks = (d_own, d_1, d_2, d_3)
    sent, kept = weights(l_blocks, d_blocks, ready)
    got = send(sent, other_core)
    key_weight, value_weight = call(
        finish_kernel, (struct((WIDTH // 2, HD), f32),) * 2, (kept, got)
    )
    return query_grad, key_weight, value_weight


def solution(mesh):
    placed = (
        P("ctx", "tp"),
        P("ctx", "tp"),
        P("ctx", "tp"),
        P("ctx", "tp"),
        P("ctx", "tp"),
        P("tp", "ctx"),
        P("ctx", "tp"),
        P(),
    )
    return jax.shard_map(
        on_device,
        mesh=mesh,
        in_specs=placed,
        out_specs=(P("ctx", "tp"), P("ctx", "tp"), P("ctx", "tp")),
        check_vma=False,
    )
```

```python
import functools
import itertools
import math

import jax
import jax.numpy as jnp
from jax import lax
from jax.experimental import pallas as pl
from jax.experimental.pallas import tpu as pltpu
from jax.sharding import PartitionSpec as P

HD = 128
HEADS = 8
ROWS = 256
WIDTH = HEADS * HD
SCALE = 1.0 / math.sqrt(HD)
LOG2E = math.log2(math.e)
AXES = ("ctx", "tp")
DOCS = 16
STEP_HEADS = 8
GROUP = 16

f32 = jnp.float32
bf16 = jnp.bfloat16


def linear(x, y, z, core):
    zh, zl = divmod(z, 2)
    return ((y * 2 + zl) * 2 + core) * 8 + x * 2 + zh


def route(target):
    pairs = []
    for x, y, z, core in itertools.product(range(4), range(4), range(4), range(2)):
        to = target(x, y, z, core)
        if to is not None:
            pairs.append((linear(x, y, z, core), linear(*to)))
    return pairs


def send(value, target):
    return lax.ppermute(value, AXES, route(target))


def other_core(x, y, z, core):
    return (x, y, z, 1 - core)


def shifted(dx=0, dy=0, dz=0):
    return lambda x, y, z, core: ((x + dx) % 4, (y + dy) % 4, (z + dz) % 4, core)


def other_zl(x, y, z, core):
    return (x, y, z ^ 1, core)


def spread(x, y, z, core):
    zh, zl = divmod(z, 2)
    return ((x + y) % 4, x, zl * 2 + zh, core)


def spread_across(x, y, z, core):
    x, y, z, core = spread(x, y, z, core)
    return (x, y, (z + 2) % 4, core)


def within_half(flip, later):
    def target(x, y, z, core):
        place = (y % 2) * 2 + z % 2
        to = place ^ flip
        if (to > place) != later:
            return None
        return (x, y - y % 2 + to // 2, z - z % 2 + to % 2, core)

    return target


def nt(a, b):
    return lax.dot_general(a, b, (((1,), (1,)), ((), ())), preferred_element_type=f32)


def nn(a, b):
    return lax.dot_general(a, b, (((1,), (0,)), ((), ())), preferred_element_type=f32)


def tn(a, b):
    return lax.dot_general(a, b, (((0,), (0,)), ((), ())), preferred_element_type=f32)


def together(*arrays):
    return lax.optimization_barrier(arrays)


def call(kernel, out_shape, operands, megabytes=12, micros=0.01, **more):
    return pl.pallas_call(
        kernel,
        out_shape=out_shape,
        compiler_params=pltpu.CompilerParams(vmem_limit_bytes=megabytes << 20),
        cost_estimate=pl.CostEstimate(flops=int(micros * 1.15e9), bytes_accessed=1 << 16, transcendentals=0),
        **more,
    )(*operands)


def struct(shape, dtype):
    return jax.ShapeDtypeStruct(shape, dtype)


def arrived_kernel(*refs):
    refs[-1][...] = jnp.zeros_like(refs[-1])


def arrived(arrays, micros):
    return call(
        arrived_kernel,
        struct((8, 128), f32),
        arrays,
        micros=micros,
        in_specs=[pl.BlockSpec(memory_space=pl.ANY)] * len(arrays),
    )


def prepare_kernel(lengths_ref, k_any, v_any, do_any, out_any, ln_any, kv_ref, aux_ref, do_ref, out_ref, sems):
    copies = [
        pltpu.make_async_copy(src, dst, sems.at[i])
        for i, (src, dst) in enumerate(
            (
                (k_any, kv_ref.at[:, :HD]),
                (v_any, kv_ref.at[:, HD:]),
                (ln_any, aux_ref.at[HEADS : 2 * HEADS, :]),
                (do_any, do_ref),
                (out_any, out_ref),
            )
        )
    ]
    for copy in copies:
        copy.start()
    positions = lax.axis_index("ctx") * ROWS + lax.broadcasted_iota(jnp.int32, (HEADS, ROWS), 1)
    end = jnp.int32(0)
    first = jnp.zeros((HEADS, ROWS), jnp.int32)
    for i in range(DOCS):
        end = end + lengths_ref[i]
        first = jnp.where(positions >= end, end, first)
    aux_ref[2 * HEADS :, :] = first.astype(f32)
    for copy in copies:
        copy.wait()
    aux_ref[HEADS : 2 * HEADS, :] = aux_ref[HEADS : 2 * HEADS, :] * LOG2E
    for h in range(HEADS):
        cols = slice(h * HD, (h + 1) * HD)
        prod = do_ref[:, cols].astype(f32) * out_ref[:, cols].astype(f32)
        aux_ref[h : h + 1, :] = jnp.sum(prod.T, axis=0, keepdims=True)


def prepare(doc_lengths, k, v, do, out, ln):
    return call(
        prepare_kernel,
        (struct((ROWS, 2 * HD), bf16), struct((3 * HEADS, ROWS), f32)),
        (doc_lengths, k, v, do, out, ln),
        in_specs=[pl.BlockSpec(memory_space=pltpu.SMEM)] + [pl.BlockSpec(memory_space=pltpu.HBM)] * 5,
        megabytes=56,
        micros=0.3,
        scratch_shapes=[pltpu.VMEM((ROWS, WIDTH), bf16)] * 2 + [pltpu.SemaphoreType.DMA((5,))],
    )


def attention_kernel(flips, has_sum, *refs):
    refs = list(refs)
    take = lambda n: [refs.pop(0) for _ in range(n)]
    kv_refs, aux_refs, q_refs, do_refs = take(len(flips)), take(2), take(2), take(2)
    sums = take(2) if has_sum else None
    dq_refs = take(2)
    dkv_ref, dk_acc, dv_acc = refs
    me = lax.axis_index("ctx")
    dk_acc[...] = jnp.zeros_like(dk_acc)
    dv_acc[...] = jnp.zeros_like(dv_acc)

    @pl.loop(0, HEADS // STEP_HEADS)
    def _(step):
        k = jnp.concatenate([r[:, :HD] for r in kv_refs], axis=0)
        v = jnp.concatenate([r[:, HD:] for r in kv_refs], axis=0)
        offset = lax.broadcasted_iota(jnp.int32, (ROWS, 1), 0)
        key_pos = jnp.concatenate([(me ^ flip) * ROWS + offset for flip in flips], axis=0)
        lane = lax.broadcasted_iota(jnp.int32, (1, ROWS), 1)
        tiles = []
        for i in range(2):
            query_pos = (me ^ i) * ROWS + lane
            first = aux_refs[i][2 * HEADS : 2 * HEADS + 1, :].astype(jnp.int32)
            visible = (key_pos <= query_pos) & (key_pos >= first)
            for j in range(STEP_HEADS):
                h = step * STEP_HEADS + j
                cols = pl.ds(pl.multiple_of(h * HD, HD), HD)
                dots = aux_refs[i][pl.ds(h, 1), :]
                norm = aux_refs[i][pl.ds(HEADS + h, 1), :]
                tiles.append((i, cols, visible, dots, norm))
        dk = dv = None
        for start in range(0, len(tiles), GROUP):
            group = tiles[start : start + GROUP]
            products = []
            for i, cols, *_ in group:
                q, do = q_refs[i][:, cols], do_refs[i][:, cols]
                products.append((q, do, nt(k, q), nt(v, do)))
            low = []
            for (_, _, visible, dots, norm), (_, _, score, prob_grad) in zip(group, products):
                p = jnp.where(visible, jnp.exp2(score * (SCALE * LOG2E) - norm), 0.0)
                low.append((p.astype(bf16), (p * (prob_grad - dots)).astype(bf16)))
            for (i, cols, *_), (q, do, *_), (p, ds) in zip(group, products, low):
                dv_term, dk_term, dq = nn(p, do), nn(ds, q), tn(ds, k)
                dv = dv_term if dv is None else dv + dv_term
                dk = dk_term if dk is None else dk + dk_term
                if has_sum:
                    dq = dq + sums[i][:, cols]
                dq_refs[i][:, cols] = dq.astype(dq_refs[i].dtype)
        dk_acc[...] += dk
        dv_acc[...] += dv

    dkv_ref[:, :HD] = dk_acc[...].astype(dkv_ref.dtype)
    dkv_ref[:, HD:] = dv_acc[...].astype(dkv_ref.dtype)


def attention(flips, kv, aux, q, do, sums, dq_types, dkv_type, micros):
    keys = len(flips) * ROWS
    return call(
        functools.partial(attention_kernel, flips, sums is not None),
        (
            struct((ROWS, WIDTH), dq_types[0]),
            struct((ROWS, WIDTH), dq_types[1]),
            struct((keys, 2 * HD), dkv_type),
        ),
        [*kv, *aux, *q, *do, *(sums or ())],
        megabytes=24,
        micros=micros,
        scratch_shapes=[pltpu.VMEM((keys, HD), f32)] * 2,
    )


def add_kernel(own_ref, zl_ref, got_ref, sum_ref, low_ref):
    for half, near_ref in enumerate((own_ref, zl_ref)):
        rows = slice(half * ROWS, (half + 1) * ROWS)
        total = near_ref[...] + got_ref[rows, :].astype(f32)
        sum_ref[rows, :] = total
        low_ref[rows, :] = total.astype(bf16)


def close_kernel(sum_ref, got_ref, _, d_ref):
    for half in range(2):
        mine = slice(half * ROWS, (half + 1) * ROWS)
        its = slice((1 - half) * ROWS, (2 - half) * ROWS)
        total = sum_ref[mine, :] + got_ref[its, :].astype(f32)
        k_grad = (total[:, :HD] * SCALE).T.astype(bf16)
        v_grad = total[:, HD:].T.astype(bf16)
        d_ref[half * 2 * HD : half * 2 * HD + HD, :] = k_grad
        d_ref[half * 2 * HD + HD : (half + 1) * 2 * HD, :] = v_grad


def weights_kernel(*refs):
    l_refs, d_refs, (_, sent_ref, kept_ref, d_all) = refs[:8], refs[8:12], refs[12:]
    me, tp = lax.axis_index("ctx"), lax.axis_index("tp")
    core, zl, y = me % 2, (me // 2) % 2, me // 4
    x, zh = tp // 2, tp % 2
    for r in range(4):
        d_all[r] = d_refs[r][...]
    half_width = WIDTH // 2
    for out_ref, whose in ((sent_ref, 1 - core), (kept_ref, core)):
        for t in range(2):
            tile = half_width // 2
            cols = pl.ds(pl.multiple_of(whose * half_width + t * tile, tile), tile)
            total = None
            for s in range(4):
                for j in range(2):
                    rows = pl.ds(pl.multiple_of(((zh ^ j) ^ zl) * 2 * HD, 2 * HD), 2 * HD)
                    term = nn(d_all[(x + s + 2 * y) % 4, rows, :], l_refs[s * 2 + j][:, cols])
                    total = term if total is None else total + term
            out_ref[:, t * tile : (t + 1) * tile] = total


def weights(l_blocks, d_blocks, ready):
    return call(
        weights_kernel,
        (struct((2 * HD, WIDTH // 2), f32),) * 2,
        (*l_blocks, *d_blocks, ready),
        scratch_shapes=[pltpu.VMEM((4, 4 * HD, ROWS), bf16)],
    )


def finish_kernel(mine_ref, got_ref, k_ref, v_ref):
    total = mine_ref[...] + got_ref[...]
    k_ref[...] = total[:HD, :].T
    v_ref[...] = total[HD:, :].T


def on_device(queries, key_states, value_states, attn_output, output_grad, log_norms, layer_input, doc_lengths):
    q_par, do_par = (send(a, other_core) for a in (queries, output_grad))
    l_own = send(layer_input, spread)
    kv, aux_own = prepare(doc_lengths, key_states, value_states, output_grad, attn_output, log_norms)
    kv, aux_own, q_par, do_par = together(kv, aux_own, q_par, do_par)
    layer_late, kv = together(layer_input, kv)
    other_0 = send(layer_late, spread_across)
    aux_par = send(aux_own, other_core)
    kv, aux_par = together(kv, aux_par)
    aux, q, do = (aux_own, aux_par), (queries, q_par), (output_grad, do_par)

    kv_far, kv_y, kv_zl = (send(kv, within_half(flip, True)) for flip in (3, 2, 1))

    behind, ahead = shifted(dx=-1), shifted(dx=1)
    *dqs, dkv_own = attention((0,), (kv,), aux, q, do, None, (f32, f32), f32, 0.3)
    l_own, dkv_own, kv_y, kv_far, kv_zl, *dqs = together(l_own, dkv_own, kv_y, kv_far, kv_zl, *dqs)
    own_1, own_3 = send(l_own, behind), send(l_own, ahead)

    *dqs, dkv_far = attention((4, 6), (kv_y, kv_far), aux, q, do, dqs, (f32, f32), bf16, 0.3)
    got_far = send(dkv_far, within_half(2, False))
    other_0, *dqs = together(other_0, *dqs)
    other_3, other_1 = send(other_0, ahead), send(other_0, behind)
    dq_own, dq_par, dkv_zl = attention((2,), (kv_zl,), aux, q, do, dqs, (f32, bf16), f32, 1.5)
    own_1, own_3, l_own, got_far, dkv_zl, dq_own, dq_par = together(
        own_1, own_3, l_own, got_far, dkv_zl, dq_own, dq_par
    )

    pair = (2 * ROWS, 2 * HD)
    dkv, dkv_low = call(add_kernel, (struct(pair, f32), struct(pair, bf16)), (dkv_own, dkv_zl, got_far))
    got_zl = send(dkv_low, other_zl)
    dq_par, _ = together(dq_par, dkv_low)
    dq_got = send(dq_par, other_core)
    query_grad = ((dq_own + dq_got.astype(f32)) * SCALE).astype(bf16)
    early = arrived((other_1, other_3), 8)
    got_zl, query_grad = together(got_zl, query_grad)
    d_own = call(close_kernel, struct((4 * HD, ROWS), bf16), (dkv, got_zl, early))
    d_2, d_1, d_3 = (send(d_own, shifted(dy=-dy)) for dy in (2, 1, 3))
    ready = arrived((d_1, d_2, d_3), 8)

    other_3, other_1, own_1, _ = together(other_3, other_1, own_1, d_own)
    own_2, other_2 = send(own_1, behind), send(other_3, ahead)
    l_blocks = (l_own, other_0, own_1, other_1, own_2, other_2, own_3, other_3)
    d_blocks = (d_own, d_1, d_2, d_3)
    sent, kept = weights(l_blocks, d_blocks, ready)
    got = send(sent, other_core)
    key_weight, value_weight = call(
        finish_kernel, (struct((WIDTH // 2, HD), f32),) * 2, (kept, got)
    )
    return query_grad, key_weight, value_weight


def solution(mesh):
    placed = (
        P("ctx", "tp"),
        P("ctx", "tp"),
        P("ctx", "tp"),
        P("ctx", "tp"),
        P("ctx", "tp"),
        P("tp", "ctx"),
        P("ctx", "tp"),
        P(),
    )
    return jax.shard_map(
        on_device,
        mesh=mesh,
        in_specs=placed,
        out_specs=(P("ctx", "tp"), P("ctx", "tp"), P("ctx", "tp")),
        check_vma=False,
    )
```

```python
import functools
import itertools
import math

import jax
import jax.numpy as jnp
from jax import lax
from jax.experimental import pallas as pl
from jax.experimental.pallas import tpu as pltpu
from jax.sharding import PartitionSpec as P

HD = 128
HEADS = 8
ROWS = 256
WIDTH = HEADS * HD
SCALE = 1.0 / math.sqrt(HD)
LOG2E = math.log2(math.e)
AXES = ("ctx", "tp")
DOCS = 16
STEP_HEADS = 8
GROUP = 16

f32 = jnp.float32
bf16 = jnp.bfloat16


def linear(x, y, z, core):
    zh, zl = divmod(z, 2)
    return ((y * 2 + zl) * 2 + core) * 8 + x * 2 + zh


def route(target):
    pairs = []
    for x, y, z, core in itertools.product(range(4), range(4), range(4), range(2)):
        to = target(x, y, z, core)
        if to is not None:
            pairs.append((linear(x, y, z, core), linear(*to)))
    return pairs


def send(value, target):
    return lax.ppermute(value, AXES, route(target))


def other_core(x, y, z, core):
    return (x, y, z, 1 - core)


def shifted(dx=0, dy=0, dz=0):
    return lambda x, y, z, core: ((x + dx) % 4, (y + dy) % 4, (z + dz) % 4, core)


def other_zl(x, y, z, core):
    return (x, y, z ^ 1, core)


def spread(x, y, z, core):
    zh, zl = divmod(z, 2)
    return ((x + y) % 4, x, zl * 2 + zh, core)


def within_half(flip, later):
    def target(x, y, z, core):
        place = (y % 2) * 2 + z % 2
        to = place ^ flip
        if (to > place) != later:
            return None
        return (x, y - y % 2 + to // 2, z - z % 2 + to % 2, core)

    return target


def nt(a, b):
    return lax.dot_general(a, b, (((1,), (1,)), ((), ())), preferred_element_type=f32)


def nn(a, b):
    return lax.dot_general(a, b, (((1,), (0,)), ((), ())), preferred_element_type=f32)


def tn(a, b):
    return lax.dot_general(a, b, (((0,), (0,)), ((), ())), preferred_element_type=f32)


def together(*arrays):
    return lax.optimization_barrier(arrays)


def call(kernel, out_shape, operands, megabytes=12, micros=0.01, **more):
    return pl.pallas_call(
        kernel,
        out_shape=out_shape,
        compiler_params=pltpu.CompilerParams(vmem_limit_bytes=megabytes << 20),
        cost_estimate=pl.CostEstimate(flops=int(micros * 1.15e9), bytes_accessed=1 << 16, transcendentals=0),
        **more,
    )(*operands)


def struct(shape, dtype):
    return jax.ShapeDtypeStruct(shape, dtype)


def arrived_kernel(*refs):
    refs[-1][...] = jnp.zeros_like(refs[-1])


def arrived(arrays, micros):
    return call(
        arrived_kernel,
        struct((8, 128), f32),
        arrays,
        micros=micros,
        in_specs=[pl.BlockSpec(memory_space=pl.ANY)] * len(arrays),
    )


def prepare_kernel(lengths_ref, k_any, v_any, do_any, out_any, ln_any, kv_ref, aux_ref, do_ref, out_ref, sems):
    copies = [
        pltpu.make_async_copy(src, dst, sems.at[i])
        for i, (src, dst) in enumerate(
            (
                (k_any, kv_ref.at[:, :HD]),
                (v_any, kv_ref.at[:, HD:]),
                (ln_any, aux_ref.at[HEADS : 2 * HEADS, :]),
                (do_any, do_ref),
                (out_any, out_ref),
            )
        )
    ]
    for copy in copies:
        copy.start()
    positions = lax.axis_index("ctx") * ROWS + lax.broadcasted_iota(jnp.int32, (HEADS, ROWS), 1)
    end = jnp.int32(0)
    first = jnp.zeros((HEADS, ROWS), jnp.int32)
    for i in range(DOCS):
        end = end + lengths_ref[i]
        first = jnp.where(positions >= end, end, first)
    aux_ref[2 * HEADS :, :] = first.astype(f32)
    for copy in copies:
        copy.wait()
    aux_ref[HEADS : 2 * HEADS, :] = aux_ref[HEADS : 2 * HEADS, :] * LOG2E
    for h in range(HEADS):
        cols = slice(h * HD, (h + 1) * HD)
        prod = do_ref[:, cols].astype(f32) * out_ref[:, cols].astype(f32)
        aux_ref[h : h + 1, :] = jnp.sum(prod.T, axis=0, keepdims=True)


def prepare(doc_lengths, k, v, do, out, ln):
    return call(
        prepare_kernel,
        (struct((ROWS, 2 * HD), bf16), struct((3 * HEADS, ROWS), f32)),
        (doc_lengths, k, v, do, out, ln),
        in_specs=[pl.BlockSpec(memory_space=pltpu.SMEM)] + [pl.BlockSpec(memory_space=pltpu.HBM)] * 5,
        megabytes=56,
        micros=0.3,
        scratch_shapes=[pltpu.VMEM((ROWS, WIDTH), bf16)] * 2 + [pltpu.SemaphoreType.DMA((5,))],
    )


def attention_kernel(flips, has_sum, *refs):
    refs = list(refs)
    take = lambda n: [refs.pop(0) for _ in range(n)]
    kv_refs, aux_refs, q_refs, do_refs = take(len(flips)), take(2), take(2), take(2)
    sums = take(2) if has_sum else None
    dq_refs = take(2)
    dkv_ref, dk_acc, dv_acc = refs
    me = lax.axis_index("ctx")
    dk_acc[...] = jnp.zeros_like(dk_acc)
    dv_acc[...] = jnp.zeros_like(dv_acc)

    @pl.loop(0, HEADS // STEP_HEADS)
    def _(step):
        k = jnp.concatenate([r[:, :HD] for r in kv_refs], axis=0)
        v = jnp.concatenate([r[:, HD:] for r in kv_refs], axis=0)
        offset = lax.broadcasted_iota(jnp.int32, (ROWS, 1), 0)
        key_pos = jnp.concatenate([(me ^ flip) * ROWS + offset for flip in flips], axis=0)
        lane = lax.broadcasted_iota(jnp.int32, (1, ROWS), 1)
        tiles = []
        for i in range(2):
            query_pos = (me ^ i) * ROWS + lane
            first = aux_refs[i][2 * HEADS : 2 * HEADS + 1, :].astype(jnp.int32)
            visible = (key_pos <= query_pos) & (key_pos >= first)
            for j in range(STEP_HEADS):
                h = step * STEP_HEADS + j
                cols = pl.ds(pl.multiple_of(h * HD, HD), HD)
                dots = aux_refs[i][pl.ds(h, 1), :]
                norm = aux_refs[i][pl.ds(HEADS + h, 1), :]
                tiles.append((i, cols, visible, dots, norm))
        dk = dv = None
        for start in range(0, len(tiles), GROUP):
            group = tiles[start : start + GROUP]
            products = []
            for i, cols, *_ in group:
                q, do = q_refs[i][:, cols], do_refs[i][:, cols]
                products.append((q, do, nt(k, q), nt(v, do)))
            low = []
            for (_, _, visible, dots, norm), (_, _, score, prob_grad) in zip(group, products):
                p = jnp.where(visible, jnp.exp2(score * (SCALE * LOG2E) - norm), 0.0)
                low.append((p.astype(bf16), (p * (prob_grad - dots)).astype(bf16)))
            for (i, cols, *_), (q, do, *_), (p, ds) in zip(group, products, low):
                dv_term, dk_term, dq = nn(p, do), nn(ds, q), tn(ds, k)
                dv = dv_term if dv is None else dv + dv_term
                dk = dk_term if dk is None else dk + dk_term
                if has_sum:
                    dq = dq + sums[i][:, cols]
                dq_refs[i][:, cols] = dq.astype(dq_refs[i].dtype)
        dk_acc[...] += dk
        dv_acc[...] += dv

    dkv_ref[:, :HD] = dk_acc[...].astype(dkv_ref.dtype)
    dkv_ref[:, HD:] = dv_acc[...].astype(dkv_ref.dtype)


def attention(flips, kv, aux, q, do, sums, dq_types, dkv_type, micros):
    keys = len(flips) * ROWS
    return call(
        functools.partial(attention_kernel, flips, sums is not None),
        (
            struct((ROWS, WIDTH), dq_types[0]),
            struct((ROWS, WIDTH), dq_types[1]),
            struct((keys, 2 * HD), dkv_type),
        ),
        [*kv, *aux, *q, *do, *(sums or ())],
        megabytes=24,
        micros=micros,
        scratch_shapes=[pltpu.VMEM((keys, HD), f32)] * 2,
    )


def add_kernel(own_ref, zl_ref, got_ref, _, sum_ref, low_ref):
    for half, near_ref in enumerate((own_ref, zl_ref)):
        rows = slice(half * ROWS, (half + 1) * ROWS)
        total = near_ref[...] + got_ref[rows, :].astype(f32)
        sum_ref[rows, :] = total
        low_ref[rows, :] = total.astype(bf16)


def close_kernel(sum_ref, got_ref, _, d_ref):
    for half in range(2):
        mine = slice(half * ROWS, (half + 1) * ROWS)
        its = slice((1 - half) * ROWS, (2 - half) * ROWS)
        total = sum_ref[mine, :] + got_ref[its, :].astype(f32)
        k_grad = (total[:, :HD] * SCALE).T.astype(bf16)
        v_grad = total[:, HD:].T.astype(bf16)
        d_ref[half * 2 * HD : half * 2 * HD + HD, :] = k_grad
        d_ref[half * 2 * HD + HD : (half + 1) * 2 * HD, :] = v_grad


def weights_kernel(*refs):
    l_refs, d_refs, (_, sent_ref, kept_ref, d_all) = refs[:8], refs[8:12], refs[12:]
    me, tp = lax.axis_index("ctx"), lax.axis_index("tp")
    core, zl, y = me % 2, (me // 2) % 2, me // 4
    x, zh = tp // 2, tp % 2
    for r in range(4):
        d_all[r] = d_refs[r][...]
    half_width = WIDTH // 2
    for out_ref, whose in ((sent_ref, 1 - core), (kept_ref, core)):
        for t in range(2):
            tile = half_width // 2
            cols = pl.ds(pl.multiple_of(whose * half_width + t * tile, tile), tile)
            total = None
            for s in range(4):
                for j in range(2):
                    rows = pl.ds(pl.multiple_of(((zh ^ j) ^ zl) * 2 * HD, 2 * HD), 2 * HD)
                    term = nn(d_all[(x + s + 2 * y) % 4, rows, :], l_refs[s * 2 + j][:, cols])
                    total = term if total is None else total + term
            out_ref[:, t * tile : (t + 1) * tile] = total


def weights(l_blocks, d_blocks, ready):
    return call(
        weights_kernel,
        (struct((2 * HD, WIDTH // 2), f32),) * 2,
        (*l_blocks, *d_blocks, ready),
        scratch_shapes=[pltpu.VMEM((4, 4 * HD, ROWS), bf16)],
    )


def finish_kernel(mine_ref, got_ref, k_ref, v_ref):
    total = mine_ref[...] + got_ref[...]
    k_ref[...] = total[:HD, :].T
    v_ref[...] = total[HD:, :].T


def on_device(queries, key_states, value_states, attn_output, output_grad, log_norms, layer_input, doc_lengths):
    q_par, do_par = (send(a, other_core) for a in (queries, output_grad))
    l_own = send(layer_input, spread)
    kv, aux_own = prepare(doc_lengths, key_states, value_states, output_grad, attn_output, log_norms)
    kv, aux_own, q_par, do_par = together(kv, aux_own, q_par, do_par)
    aux_par = send(aux_own, other_core)
    kv, aux_par = together(kv, aux_par)
    aux, q, do = (aux_own, aux_par), (queries, q_par), (output_grad, do_par)

    kv_far, kv_y, kv_zl = (send(kv, within_half(flip, True)) for flip in (3, 2, 1))

    behind, ahead, across = shifted(dx=-1), shifted(dx=1), shifted(dz=2)
    *dqs, dkv_own = attention((0,), (kv,), aux, q, do, None, (f32, f32), f32, 0.3)
    l_own, dkv_own, kv_y, kv_far, kv_zl, *dqs = together(l_own, dkv_own, kv_y, kv_far, kv_zl, *dqs)
    other_0, own_1, own_3 = (send(l_own, t) for t in (across, behind, ahead))

    *dqs, dkv_far = attention((4, 6), (kv_y, kv_far), aux, q, do, dqs, (f32, f32), bf16, 0.3)
    got_far = send(dkv_far, within_half(2, False))
    dq_own, dq_par, dkv_zl = attention((2,), (kv_zl,), aux, q, do, dqs, (f32, bf16), f32, 1.5)
    other_0, own_1, own_3, l_own, dkv_zl = together(other_0, own_1, own_3, l_own, dkv_zl)

    other_3, other_1 = send(other_0, ahead), send(other_0, behind)
    early = arrived((other_1, other_3), 8)

    pair = (2 * ROWS, 2 * HD)
    there = arrived((got_far,), 4)
    dkv, dkv_low = call(add_kernel, (struct(pair, f32), struct(pair, bf16)), (dkv_own, dkv_zl, got_far, there))
    got_zl = send(dkv_low, other_zl)
    dq_par, _ = together(dq_par, dkv_low)
    dq_got = send(dq_par, other_core)
    query_grad = ((dq_own + dq_got.astype(f32)) * SCALE).astype(bf16)
    got_zl, query_grad, early = together(got_zl, query_grad, early)
    d_own = call(close_kernel, struct((4 * HD, ROWS), bf16), (dkv, got_zl, early))
    d_2, d_1, d_3 = (send(d_own, shifted(dy=-dy)) for dy in (2, 1, 3))
    ready = arrived((d_1, d_2, d_3), 8)

    other_3, other_1, own_1, _ = together(other_3, other_1, own_1, d_own)
    own_2, other_2 = send(own_1, behind), send(other_3, ahead)
    l_blocks = (l_own, other_0, own_1, other_1, own_2, other_2, own_3, other_3)
    d_blocks = (d_own, d_1, d_2, d_3)
    sent, kept = weights(l_blocks, d_blocks, ready)
    got = send(sent, other_core)
    key_weight, value_weight = call(
        finish_kernel, (struct((WIDTH // 2, HD), f32),) * 2, (kept, got)
    )
    return query_grad, key_weight, value_weight


def solution(mesh):
    placed = (
        P("ctx", "tp"),
        P("ctx", "tp"),
        P("ctx", "tp"),
        P("ctx", "tp"),
        P("ctx", "tp"),
        P("tp", "ctx"),
        P("ctx", "tp"),
        P(),
    )
    return jax.shard_map(
        on_device,
        mesh=mesh,
        in_specs=placed,
        out_specs=(P("ctx", "tp"), P("ctx", "tp"), P("ctx", "tp")),
        check_vma=False,
    )
```

```python
import functools
import itertools
import math

import jax
import jax.numpy as jnp
from jax import lax
from jax.experimental import pallas as pl
from jax.experimental.pallas import tpu as pltpu
from jax.sharding import PartitionSpec as P

HD = 128
HEADS = 8
ROWS = 256
WIDTH = HEADS * HD
SCALE = 1.0 / math.sqrt(HD)
LOG2E = math.log2(math.e)
AXES = ("ctx", "tp")
DOCS = 16
STEP_HEADS = 8
GROUP = 16

f32 = jnp.float32
bf16 = jnp.bfloat16


def linear(x, y, z, core):
    zh, zl = divmod(z, 2)
    return ((y * 2 + zl) * 2 + core) * 8 + x * 2 + zh


def route(target):
    pairs = []
    for x, y, z, core in itertools.product(range(4), range(4), range(4), range(2)):
        to = target(x, y, z, core)
        if to is not None:
            pairs.append((linear(x, y, z, core), linear(*to)))
    return pairs


def send(value, target):
    return lax.ppermute(value, AXES, route(target))


def other_core(x, y, z, core):
    return (x, y, z, 1 - core)


def shifted(dx=0, dy=0, dz=0):
    return lambda x, y, z, core: ((x + dx) % 4, (y + dy) % 4, (z + dz) % 4, core)


def other_zl(x, y, z, core):
    return (x, y, z ^ 1, core)


def spread(x, y, z, core):
    zh, zl = divmod(z, 2)
    return ((x + y) % 4, x, zl * 2 + zh, core)


def within_half(flip, later):
    def target(x, y, z, core):
        place = (y % 2) * 2 + z % 2
        to = place ^ flip
        if (to > place) != later:
            return None
        return (x, y - y % 2 + to // 2, z - z % 2 + to % 2, core)

    return target


def nt(a, b):
    return lax.dot_general(a, b, (((1,), (1,)), ((), ())), preferred_element_type=f32)


def nn(a, b):
    return lax.dot_general(a, b, (((1,), (0,)), ((), ())), preferred_element_type=f32)


def tn(a, b):
    return lax.dot_general(a, b, (((0,), (0,)), ((), ())), preferred_element_type=f32)


def together(*arrays):
    return lax.optimization_barrier(arrays)


def call(kernel, out_shape, operands, megabytes=12, micros=0.01, **more):
    return pl.pallas_call(
        kernel,
        out_shape=out_shape,
        compiler_params=pltpu.CompilerParams(vmem_limit_bytes=megabytes << 20),
        cost_estimate=pl.CostEstimate(flops=int(micros * 1.15e9), bytes_accessed=1 << 16, transcendentals=0),
        **more,
    )(*operands)


def struct(shape, dtype):
    return jax.ShapeDtypeStruct(shape, dtype)


def arrived_kernel(*refs):
    refs[-1][...] = jnp.zeros_like(refs[-1])


def arrived(arrays, micros):
    return call(
        arrived_kernel,
        struct((8, 128), f32),
        arrays,
        micros=micros,
        in_specs=[pl.BlockSpec(memory_space=pl.ANY)] * len(arrays),
    )


def prepare_kernel(lengths_ref, k_any, v_any, do_any, out_any, ln_any, kv_ref, aux_ref, do_ref, out_ref, sems):
    copies = [
        pltpu.make_async_copy(src, dst, sems.at[i])
        for i, (src, dst) in enumerate(
            (
                (k_any, kv_ref.at[:, :HD]),
                (v_any, kv_ref.at[:, HD:]),
                (ln_any, aux_ref.at[HEADS : 2 * HEADS, :]),
                (do_any, do_ref),
                (out_any, out_ref),
            )
        )
    ]
    for copy in copies:
        copy.start()
    positions = lax.axis_index("ctx") * ROWS + lax.broadcasted_iota(jnp.int32, (HEADS, ROWS), 1)
    end = jnp.int32(0)
    first = jnp.zeros((HEADS, ROWS), jnp.int32)
    for i in range(DOCS):
        end = end + lengths_ref[i]
        first = jnp.where(positions >= end, end, first)
    aux_ref[2 * HEADS :, :] = first.astype(f32)
    for copy in copies:
        copy.wait()
    aux_ref[HEADS : 2 * HEADS, :] = aux_ref[HEADS : 2 * HEADS, :] * LOG2E
    for h in range(HEADS):
        cols = slice(h * HD, (h + 1) * HD)
        prod = do_ref[:, cols].astype(f32) * out_ref[:, cols].astype(f32)
        aux_ref[h : h + 1, :] = jnp.sum(prod.T, axis=0, keepdims=True)


def prepare(doc_lengths, k, v, do, out, ln):
    return call(
        prepare_kernel,
        (struct((ROWS, 2 * HD), bf16), struct((3 * HEADS, ROWS), f32)),
        (doc_lengths, k, v, do, out, ln),
        in_specs=[pl.BlockSpec(memory_space=pltpu.SMEM)] + [pl.BlockSpec(memory_space=pltpu.HBM)] * 5,
        megabytes=56,
        micros=0.3,
        scratch_shapes=[pltpu.VMEM((ROWS, WIDTH), bf16)] * 2 + [pltpu.SemaphoreType.DMA((5,))],
    )


def attention_kernel(flips, has_sum, *refs):
    refs = list(refs)
    take = lambda n: [refs.pop(0) for _ in range(n)]
    kv_refs, aux_refs, q_refs, do_refs = take(len(flips)), take(2), take(2), take(2)
    sums = take(2) if has_sum else None
    dq_refs = take(2)
    dkv_ref, dk_acc, dv_acc = refs
    me = lax.axis_index("ctx")
    dk_acc[...] = jnp.zeros_like(dk_acc)
    dv_acc[...] = jnp.zeros_like(dv_acc)

    @pl.loop(0, HEADS // STEP_HEADS)
    def _(step):
        k = jnp.concatenate([r[:, :HD] for r in kv_refs], axis=0)
        v = jnp.concatenate([r[:, HD:] for r in kv_refs], axis=0)
        offset = lax.broadcasted_iota(jnp.int32, (ROWS, 1), 0)
        key_pos = jnp.concatenate([(me ^ flip) * ROWS + offset for flip in flips], axis=0)
        lane = lax.broadcasted_iota(jnp.int32, (1, ROWS), 1)
        tiles = []
        for i in range(2):
            query_pos = (me ^ i) * ROWS + lane
            first = aux_refs[i][2 * HEADS : 2 * HEADS + 1, :].astype(jnp.int32)
            visible = (key_pos <= query_pos) & (key_pos >= first)
            for j in range(STEP_HEADS):
                h = step * STEP_HEADS + j
                cols = pl.ds(pl.multiple_of(h * HD, HD), HD)
                dots = aux_refs[i][pl.ds(h, 1), :]
                norm = aux_refs[i][pl.ds(HEADS + h, 1), :]
                tiles.append((i, cols, visible, dots, norm))
        dk = dv = None
        for start in range(0, len(tiles), GROUP):
            group = tiles[start : start + GROUP]
            products = []
            for i, cols, *_ in group:
                q, do = q_refs[i][:, cols], do_refs[i][:, cols]
                products.append((q, do, nt(k, q), nt(v, do)))
            low = []
            for (_, _, visible, dots, norm), (_, _, score, prob_grad) in zip(group, products):
                p = jnp.where(visible, jnp.exp2(score * (SCALE * LOG2E) - norm), 0.0)
                low.append((p.astype(bf16), (p * (prob_grad - dots)).astype(bf16)))
            for (i, cols, *_), (q, do, *_), (p, ds) in zip(group, products, low):
                dv_term, dk_term, dq = nn(p, do), nn(ds, q), tn(ds, k)
                dv = dv_term if dv is None else dv + dv_term
                dk = dk_term if dk is None else dk + dk_term
                if has_sum:
                    dq = dq + sums[i][:, cols]
                dq_refs[i][:, cols] = dq.astype(dq_refs[i].dtype)
        dk_acc[...] += dk
        dv_acc[...] += dv

    dkv_ref[:, :HD] = dk_acc[...].astype(dkv_ref.dtype)
    dkv_ref[:, HD:] = dv_acc[...].astype(dkv_ref.dtype)


def attention(flips, kv, aux, q, do, sums, dq_types, dkv_type, micros):
    keys = len(flips) * ROWS
    return call(
        functools.partial(attention_kernel, flips, sums is not None),
        (
            struct((ROWS, WIDTH), dq_types[0]),
            struct((ROWS, WIDTH), dq_types[1]),
            struct((keys, 2 * HD), dkv_type),
        ),
        [*kv, *aux, *q, *do, *(sums or ())],
        megabytes=24,
        micros=micros,
        scratch_shapes=[pltpu.VMEM((keys, HD), f32)] * 2,
    )


def add_kernel(own_ref, zl_ref, got_ref, _, sum_ref, low_ref):
    for half, near_ref in enumerate((own_ref, zl_ref)):
        rows = slice(half * ROWS, (half + 1) * ROWS)
        total = near_ref[...] + got_ref[rows, :].astype(f32)
        sum_ref[rows, :] = total
        low_ref[rows, :] = total.astype(bf16)


def close_kernel(sum_ref, got_ref, _, d_ref):
    for half in range(2):
        mine = slice(half * ROWS, (half + 1) * ROWS)
        its = slice((1 - half) * ROWS, (2 - half) * ROWS)
        total = sum_ref[mine, :] + got_ref[its, :].astype(f32)
        k_grad = (total[:, :HD] * SCALE).T.astype(bf16)
        v_grad = total[:, HD:].T.astype(bf16)
        d_ref[half * 2 * HD : half * 2 * HD + HD, :] = k_grad
        d_ref[half * 2 * HD + HD : (half + 1) * 2 * HD, :] = v_grad


def weights_kernel(own_half, *refs):
    l_refs, d_refs, (_, out_ref, d_all) = refs[:8], refs[8:12], refs[12:]
    me, tp = lax.axis_index("ctx"), lax.axis_index("tp")
    core, zl, y = me % 2, (me // 2) % 2, me // 4
    x, zh = tp // 2, tp % 2
    for r in range(4):
        d_all[r] = d_refs[r][...]
    half_width = WIDTH // 2
    whose = core if own_half else 1 - core
    for t in range(2):
        tile = half_width // 2
        cols = pl.ds(pl.multiple_of(whose * half_width + t * tile, tile), tile)
        total = None
        for s in range(4):
            for j in range(2):
                rows = pl.ds(pl.multiple_of(((zh ^ j) ^ zl) * 2 * HD, 2 * HD), 2 * HD)
                term = nn(d_all[(x + s + 2 * y) % 4, rows, :], l_refs[s * 2 + j][:, cols])
                total = term if total is None else total + term
        out_ref[:, t * tile : (t + 1) * tile] = total


def weights(own_half, l_blocks, d_blocks, ready):
    return call(
        functools.partial(weights_kernel, own_half),
        struct((2 * HD, WIDTH // 2), f32),
        (*l_blocks, *d_blocks, ready),
        scratch_shapes=[pltpu.VMEM((4, 4 * HD, ROWS), bf16)],
    )


def finish_kernel(mine_ref, got_ref, k_ref, v_ref):
    total = mine_ref[...] + got_ref[...]
    k_ref[...] = total[:HD, :].T
    v_ref[...] = total[HD:, :].T


def on_device(queries, key_states, value_states, attn_output, output_grad, log_norms, layer_input, doc_lengths):
    q_par, do_par = (send(a, other_core) for a in (queries, output_grad))
    l_own = send(layer_input, spread)
    kv, aux_own = prepare(doc_lengths, key_states, value_states, output_grad, attn_output, log_norms)
    kv, aux_own, q_par, do_par = together(kv, aux_own, q_par, do_par)
    aux_par = send(aux_own, other_core)
    kv, aux_par = together(kv, aux_par)
    aux, q, do = (aux_own, aux_par), (queries, q_par), (output_grad, do_par)

    kv_far, kv_y, kv_zl = (send(kv, within_half(flip, True)) for flip in (3, 2, 1))

    behind, ahead, across = shifted(dx=-1), shifted(dx=1), shifted(dz=2)
    *dqs, dkv_own = attention((0,), (kv,), aux, q, do, None, (f32, f32), f32, 0.3)
    l_own, dkv_own, kv_y, kv_far, kv_zl, *dqs = together(l_own, dkv_own, kv_y, kv_far, kv_zl, *dqs)
    other_0, own_1, own_3 = (send(l_own, t) for t in (across, behind, ahead))

    *dqs, dkv_far = attention((4, 6), (kv_y, kv_far), aux, q, do, dqs, (f32, f32), bf16, 0.3)
    got_far = send(dkv_far, within_half(2, False))
    dq_own, dq_par, dkv_zl = attention((2,), (kv_zl,), aux, q, do, dqs, (f32, bf16), f32, 1.5)
    other_0, own_1, own_3, l_own, dkv_zl = together(other_0, own_1, own_3, l_own, dkv_zl)

    other_3, other_1 = send(other_0, ahead), send(other_0, behind)
    early = arrived((other_1, other_3), 8)

    pair = (2 * ROWS, 2 * HD)
    there = arrived((got_far,), 4)
    dkv, dkv_low = call(add_kernel, (struct(pair, f32), struct(pair, bf16)), (dkv_own, dkv_zl, got_far, there))
    got_zl = send(dkv_low, other_zl)
    dq_par, _ = together(dq_par, dkv_low)
    dq_got = send(dq_par, other_core)
    got_zl, dq_got, early = together(got_zl, dq_got, early)
    d_own = call(close_kernel, struct((4 * HD, ROWS), bf16), (dkv, got_zl, early))
    d_2, d_1, d_3 = (send(d_own, shifted(dy=-dy)) for dy in (2, 1, 3))
    ready = arrived((d_1, d_2, d_3), 8)

    other_3, other_1, own_1, _ = together(other_3, other_1, own_1, d_own)
    own_2, other_2 = send(own_1, behind), send(other_3, ahead)
    dq_got, d_own = together(dq_got, d_own)
    query_grad = ((dq_own + dq_got.astype(f32)) * SCALE).astype(bf16)
    l_blocks = (l_own, other_0, own_1, other_1, own_2, other_2, own_3, other_3)
    d_blocks = (d_own, d_1, d_2, d_3)
    sent = weights(False, l_blocks, d_blocks, ready)
    got = send(sent, other_core)
    kept = weights(True, l_blocks, d_blocks, ready)
    key_weight, value_weight = call(
        finish_kernel, (struct((WIDTH // 2, HD), f32),) * 2, (kept, got)
    )
    return query_grad, key_weight, value_weight


def solution(mesh):
    placed = (
        P("ctx", "tp"),
        P("ctx", "tp"),
        P("ctx", "tp"),
        P("ctx", "tp"),
        P("ctx", "tp"),
        P("tp", "ctx"),
        P("ctx", "tp"),
        P(),
    )
    return jax.shard_map(
        on_device,
        mesh=mesh,
        in_specs=placed,
        out_specs=(P("ctx", "tp"), P("ctx", "tp"), P("ctx", "tp")),
        check_vma=False,
    )
```

```python
import functools
import itertools
import math

import jax
import jax.numpy as jnp
from jax import lax
from jax.experimental import pallas as pl
from jax.experimental.pallas import tpu as pltpu
from jax.sharding import PartitionSpec as P

HD = 128
HEADS = 8
ROWS = 256
WIDTH = HEADS * HD
SCALE = 1.0 / math.sqrt(HD)
LOG2E = math.log2(math.e)
AXES = ("ctx", "tp")
DOCS = 16
STEP_HEADS = 8
GROUP = 16

f32 = jnp.float32
bf16 = jnp.bfloat16


def linear(x, y, z, core):
    zh, zl = divmod(z, 2)
    return ((y * 2 + zl) * 2 + core) * 8 + x * 2 + zh


def route(target):
    pairs = []
    for x, y, z, core in itertools.product(range(4), range(4), range(4), range(2)):
        to = target(x, y, z, core)
        if to is not None:
            pairs.append((linear(x, y, z, core), linear(*to)))
    return pairs


def send(value, target):
    return lax.ppermute(value, AXES, route(target))


def other_core(x, y, z, core):
    return (x, y, z, 1 - core)


def shifted(dx=0, dy=0, dz=0):
    return lambda x, y, z, core: ((x + dx) % 4, (y + dy) % 4, (z + dz) % 4, core)


def other_zl(x, y, z, core):
    return (x, y, z ^ 1, core)


def spread(x, y, z, core):
    zh, zl = divmod(z, 2)
    return ((x + y) % 4, x, zl * 2 + zh, core)


def within_half(flip, later):
    def target(x, y, z, core):
        place = (y % 2) * 2 + z % 2
        to = place ^ flip
        if (to > place) != later:
            return None
        return (x, y - y % 2 + to // 2, z - z % 2 + to % 2, core)

    return target


def nt(a, b):
    return lax.dot_general(a, b, (((1,), (1,)), ((), ())), preferred_element_type=f32)


def nn(a, b):
    return lax.dot_general(a, b, (((1,), (0,)), ((), ())), preferred_element_type=f32)


def tn(a, b):
    return lax.dot_general(a, b, (((0,), (0,)), ((), ())), preferred_element_type=f32)


def together(*arrays):
    return lax.optimization_barrier(arrays)


def call(kernel, out_shape, operands, megabytes=12, micros=0.01, **more):
    return pl.pallas_call(
        kernel,
        out_shape=out_shape,
        compiler_params=pltpu.CompilerParams(vmem_limit_bytes=megabytes << 20),
        cost_estimate=pl.CostEstimate(flops=int(micros * 1.15e9), bytes_accessed=1 << 16, transcendentals=0),
        **more,
    )(*operands)


def struct(shape, dtype):
    return jax.ShapeDtypeStruct(shape, dtype)


def arrived_kernel(*refs):
    refs[-1][...] = jnp.zeros_like(refs[-1])


def arrived(arrays, micros):
    return call(
        arrived_kernel,
        struct((8, 128), f32),
        arrays,
        micros=micros,
        in_specs=[pl.BlockSpec(memory_space=pl.ANY)] * len(arrays),
    )


def prepare_kernel(lengths_ref, k_any, v_any, do_any, out_any, ln_any, kv_ref, aux_ref, do_ref, out_ref, sems):
    copies = [
        pltpu.make_async_copy(src, dst, sems.at[i])
        for i, (src, dst) in enumerate(
            (
                (k_any, kv_ref.at[:, :HD]),
                (v_any, kv_ref.at[:, HD:]),
                (ln_any, aux_ref.at[HEADS : 2 * HEADS, :]),
                (do_any, do_ref),
                (out_any, out_ref),
            )
        )
    ]
    for copy in copies:
        copy.start()
    positions = lax.axis_index("ctx") * ROWS + lax.broadcasted_iota(jnp.int32, (HEADS, ROWS), 1)
    end = jnp.int32(0)
    first = jnp.zeros((HEADS, ROWS), jnp.int32)
    for i in range(DOCS):
        end = end + lengths_ref[i]
        first = jnp.where(positions >= end, end, first)
    aux_ref[2 * HEADS :, :] = first.astype(f32)
    for copy in copies:
        copy.wait()
    aux_ref[HEADS : 2 * HEADS, :] = aux_ref[HEADS : 2 * HEADS, :] * LOG2E
    for h in range(HEADS):
        cols = slice(h * HD, (h + 1) * HD)
        prod = do_ref[:, cols].astype(f32) * out_ref[:, cols].astype(f32)
        aux_ref[h : h + 1, :] = jnp.sum(prod.T, axis=0, keepdims=True)


def prepare(doc_lengths, k, v, do, out, ln):
    return call(
        prepare_kernel,
        (struct((ROWS, 2 * HD), bf16), struct((3 * HEADS, ROWS), f32)),
        (doc_lengths, k, v, do, out, ln),
        in_specs=[pl.BlockSpec(memory_space=pltpu.SMEM)] + [pl.BlockSpec(memory_space=pltpu.HBM)] * 5,
        megabytes=56,
        micros=0.3,
        scratch_shapes=[pltpu.VMEM((ROWS, WIDTH), bf16)] * 2 + [pltpu.SemaphoreType.DMA((5,))],
    )


def attention_kernel(flips, has_sum, *refs):
    refs = list(refs)
    take = lambda n: [refs.pop(0) for _ in range(n)]
    kv_refs, aux_refs, q_refs, do_refs = take(len(flips)), take(2), take(2), take(2)
    sums = take(2) if has_sum else None
    dq_refs = take(2)
    dkv_ref, dk_acc, dv_acc = refs
    me = lax.axis_index("ctx")
    dk_acc[...] = jnp.zeros_like(dk_acc)
    dv_acc[...] = jnp.zeros_like(dv_acc)

    @pl.loop(0, HEADS // STEP_HEADS)
    def _(step):
        k = jnp.concatenate([r[:, :HD] for r in kv_refs], axis=0)
        v = jnp.concatenate([r[:, HD:] for r in kv_refs], axis=0)
        offset = lax.broadcasted_iota(jnp.int32, (ROWS, 1), 0)
        key_pos = jnp.concatenate([(me ^ flip) * ROWS + offset for flip in flips], axis=0)
        lane = lax.broadcasted_iota(jnp.int32, (1, ROWS), 1)
        tiles = []
        for i in range(2):
            query_pos = (me ^ i) * ROWS + lane
            first = aux_refs[i][2 * HEADS : 2 * HEADS + 1, :].astype(jnp.int32)
            visible = (key_pos <= query_pos) & (key_pos >= first)
            for j in range(STEP_HEADS):
                h = step * STEP_HEADS + j
                cols = pl.ds(pl.multiple_of(h * HD, HD), HD)
                dots = aux_refs[i][pl.ds(h, 1), :]
                norm = aux_refs[i][pl.ds(HEADS + h, 1), :]
                tiles.append((i, cols, visible, dots, norm))
        dk = dv = None
        for start in range(0, len(tiles), GROUP):
            group = tiles[start : start + GROUP]
            products = []
            for i, cols, *_ in group:
                q, do = q_refs[i][:, cols], do_refs[i][:, cols]
                products.append((q, do, nt(k, q), nt(v, do)))
            low = []
            for (_, _, visible, dots, norm), (_, _, score, prob_grad) in zip(group, products):
                p = jnp.where(visible, jnp.exp2(score * (SCALE * LOG2E) - norm), 0.0)
                low.append((p.astype(bf16), (p * (prob_grad - dots)).astype(bf16)))
            for (i, cols, *_), (q, do, *_), (p, ds) in zip(group, products, low):
                dv_term, dk_term, dq = nn(p, do), nn(ds, q), tn(ds, k)
                dv = dv_term if dv is None else dv + dv_term
                dk = dk_term if dk is None else dk + dk_term
                if has_sum:
                    dq = dq + sums[i][:, cols]
                dq_refs[i][:, cols] = dq.astype(dq_refs[i].dtype)
        dk_acc[...] += dk
        dv_acc[...] += dv

    dkv_ref[:, :HD] = dk_acc[...].astype(dkv_ref.dtype)
    dkv_ref[:, HD:] = dv_acc[...].astype(dkv_ref.dtype)


def attention(flips, kv, aux, q, do, sums, dq_types, dkv_type, micros):
    keys = len(flips) * ROWS
    return call(
        functools.partial(attention_kernel, flips, sums is not None),
        (
            struct((ROWS, WIDTH), dq_types[0]),
            struct((ROWS, WIDTH), dq_types[1]),
            struct((keys, 2 * HD), dkv_type),
        ),
        [*kv, *aux, *q, *do, *(sums or ())],
        megabytes=24,
        micros=micros,
        scratch_shapes=[pltpu.VMEM((keys, HD), f32)] * 2,
    )


def add_kernel(own_ref, zl_ref, got_ref, _, sum_ref, low_ref):
    for half, near_ref in enumerate((own_ref, zl_ref)):
        rows = slice(half * ROWS, (half + 1) * ROWS)
        total = near_ref[...] + got_ref[rows, :].astype(f32)
        sum_ref[rows, :] = total
        low_ref[rows, :] = total.astype(bf16)


def close_kernel(sum_ref, got_ref, _, d_ref):
    for half in range(2):
        mine = slice(half * ROWS, (half + 1) * ROWS)
        its = slice((1 - half) * ROWS, (2 - half) * ROWS)
        total = sum_ref[mine, :] + got_ref[its, :].astype(f32)
        k_grad = (total[:, :HD] * SCALE).T.astype(bf16)
        v_grad = total[:, HD:].T.astype(bf16)
        d_ref[half * 2 * HD : half * 2 * HD + HD, :] = k_grad
        d_ref[half * 2 * HD + HD : (half + 1) * 2 * HD, :] = v_grad


def weights_kernel(own_half, *refs):
    l_refs, d_refs, (_, out_ref, d_all) = refs[:8], refs[8:12], refs[12:]
    me, tp = lax.axis_index("ctx"), lax.axis_index("tp")
    core, zl, y = me % 2, (me // 2) % 2, me // 4
    x, zh = tp // 2, tp % 2
    for r in range(4):
        d_all[r] = d_refs[r][...]
    half_width = WIDTH // 2
    whose = core if own_half else 1 - core
    for t in range(2):
        tile = half_width // 2
        cols = pl.ds(pl.multiple_of(whose * half_width + t * tile, tile), tile)
        total = None
        for s in range(4):
            for j in range(2):
                rows = pl.ds(pl.multiple_of(((zh ^ j) ^ zl) * 2 * HD, 2 * HD), 2 * HD)
                term = nn(d_all[(x + s + 2 * y) % 4, rows, :], l_refs[s * 2 + j][:, cols])
                total = term if total is None else total + term
        out_ref[:, t * tile : (t + 1) * tile] = total


def weights(own_half, l_blocks, d_blocks, ready):
    return call(
        functools.partial(weights_kernel, own_half),
        struct((2 * HD, WIDTH // 2), f32),
        (*l_blocks, *d_blocks, ready),
        scratch_shapes=[pltpu.VMEM((4, 4 * HD, ROWS), bf16)],
    )


def finish_kernel(mine_ref, got_ref, k_ref, v_ref):
    total = mine_ref[...] + got_ref[...]
    k_ref[...] = total[:HD, :].T
    v_ref[...] = total[HD:, :].T


def on_device(queries, key_states, value_states, attn_output, output_grad, log_norms, layer_input, doc_lengths):
    q_par, do_par = (send(a, other_core) for a in (queries, output_grad))
    l_own = send(layer_input, spread)
    kv, aux_own = prepare(doc_lengths, key_states, value_states, output_grad, attn_output, log_norms)
    kv, aux_own, q_par, do_par = together(kv, aux_own, q_par, do_par)
    aux_par = send(aux_own, other_core)
    kv, aux_par = together(kv, aux_par)
    aux, q, do = (aux_own, aux_par), (queries, q_par), (output_grad, do_par)

    kv_far, kv_y, kv_zl = (send(kv, within_half(flip, True)) for flip in (3, 2, 1))

    behind, ahead, across = shifted(dx=-1), shifted(dx=1), shifted(dz=2)
    *dqs, dkv_own = attention((0,), (kv,), aux, q, do, None, (f32, f32), f32, 0.3)
    l_own, dkv_own, kv_y, kv_far, kv_zl, *dqs = together(l_own, dkv_own, kv_y, kv_far, kv_zl, *dqs)
    other_0, own_1, own_3 = (send(l_own, t) for t in (across, behind, ahead))

    *dqs, dkv_far = attention((4, 6), (kv_y, kv_far), aux, q, do, dqs, (f32, f32), bf16, 0.3)
    got_far = send(dkv_far, within_half(2, False))
    dq_own, dq_par, dkv_zl = attention((2,), (kv_zl,), aux, q, do, dqs, (f32, bf16), f32, 1.5)
    other_0, own_1, own_3, l_own, dkv_zl = together(other_0, own_1, own_3, l_own, dkv_zl)

    other_3, other_1 = send(other_0, ahead), send(other_0, behind)
    early = arrived((other_3,), 8)

    pair = (2 * ROWS, 2 * HD)
    there = arrived((got_far,), 4)
    dkv, dkv_low = call(add_kernel, (struct(pair, f32), struct(pair, bf16)), (dkv_own, dkv_zl, got_far, there))
    got_zl = send(dkv_low, other_zl)
    dq_par, _ = together(dq_par, dkv_low)
    dq_got = send(dq_par, other_core)
    got_zl, dq_got, early = together(got_zl, dq_got, early)
    d_own = call(close_kernel, struct((4 * HD, ROWS), bf16), (dkv, got_zl, early))
    d_2, d_1, d_3 = (send(d_own, shifted(dy=-dy)) for dy in (2, 1, 3))
    ready = arrived((d_1, d_2, d_3), 8)

    other_3, other_1, own_1, _ = together(other_3, other_1, own_1, d_own)
    own_2, other_2 = send(own_1, behind), send(other_3, ahead)
    dq_got, d_own = together(dq_got, d_own)
    query_grad = ((dq_own + dq_got.astype(f32)) * SCALE).astype(bf16)
    l_blocks = (l_own, other_0, own_1, other_1, own_2, other_2, own_3, other_3)
    d_blocks = (d_own, d_1, d_2, d_3)
    sent = weights(False, l_blocks, d_blocks, ready)
    got = send(sent, other_core)
    kept = weights(True, l_blocks, d_blocks, ready)
    key_weight, value_weight = call(
        finish_kernel, (struct((WIDTH // 2, HD), f32),) * 2, (kept, got)
    )
    return query_grad, key_weight, value_weight


def solution(mesh):
    placed = (
        P("ctx", "tp"),
        P("ctx", "tp"),
        P("ctx", "tp"),
        P("ctx", "tp"),
        P("ctx", "tp"),
        P("tp", "ctx"),
        P("ctx", "tp"),
        P(),
    )
    return jax.shard_map(
        on_device,
        mesh=mesh,
        in_specs=placed,
        out_specs=(P("ctx", "tp"), P("ctx", "tp"), P("ctx", "tp")),
        check_vma=False,
    )
```
